256 devices in a mesh: tm: 8 (over z_lo, core), space: 32 (over z_hi, x, y).
Axes of the slice: x: 4, y: 4, z: 8 (z_hi: 2, z_lo: 4; z = z_hi * 4 + z_lo), core: 2. Of those that a mesh axis runs over, the one named last changes fastest.
Arguments:
- trajectory: bfloat16 [32, 8, 128, 32, 128], P('tm', None, 'space'), may hold values from -6 to 6
- noise: bfloat16 [32, 8, 128, 32, 128], P('tm', None, 'space'), may hold values from -6 to 6
- start: float32 [8, 128, 32, 128], P(None, 'space'), may hold values from -6 to 6
- conv_weight: bfloat16 [27, 64, 8], replicated, may hold values from -0.4375 to 0.4375
- conv_bias: float32 [64], replicated, may hold values from -3 to 3
- step_embed: float32 [32, 64], P('tm'), may hold values from -3 to 3
- out_weight: bfloat16 [8, 64], replicated, may hold values from -0.375 to 0.375
- decoder: float32 [8], replicated, may hold values from -2 to 2
- angle_index: int32 [32], replicated, may hold values from 0 to 179
- measured: float32 [96, 32, 128], P('space'), may hold values from -6 to 6
- step_scale: float32 [32], P('tm'), may hold values from 0.03 to 0.09
- guide_scale: float32 [32], P('tm'), may hold values from 1 to 3
- noise_scale: float32 [32], P('tm'), may hold values from 0.05 to 0.2
Outputs:
- new_trajectory: float32 [32, 8, 128, 32, 128], P('tm', None, 'space')
The draws below stay inside these ranges and needn't reach their ends.
All inputs are finite; a program needn't handle non-finite values.
Results may differ from the reference program's by a relative error of at most 0.00065.
Values may be sent and summed in bfloat16 or wider, within the bound.
No kernel may reach another device: no remote copies, remote signals or barrier semaphores. Data moves between devices by JAX's collectives and lax.ppermute only.
A program may use at most 192 MiB of HBM per device.

```python
import math
import jax
import jax.numpy as jnp
from jax import lax

C = 8
H = 64
GX = 128
GY = 32
NV = 32
ANGLES = 180
STEPS = 32
NZ = 128
NS = 96


def with_ends(drawn, own_key, least, largest):
    index_at = [jax.random.randint(jax.random.fold_in(own_key, axis), (), 0, length) for axis, length in enumerate(drawn.shape)]
    longest = drawn.shape.index(max(drawn.shape))
    next_to = index_at[:longest] + [(index_at[longest] + 1) % drawn.shape[longest]] + index_at[longest + 1:]
    return drawn.at[tuple(index_at)].set(least).at[tuple(next_to)].set(largest)


def steps_of(rng, dims, cuts, low, high):
    def one(position, blocks):
        draws = jax.random.uniform(jax.random.fold_in(jax.random.fold_in(rng, 6), position), (blocks,), jnp.float32, low / len(cuts), high / len(cuts))
        return jnp.repeat(jnp.exp(draws), dims[position] // blocks).reshape((-1,) + (1,) * (len(dims) - position - 1))

    factor_of = one(*cuts[0])
    for cut in cuts[1:]:
        factor_of = factor_of * one(*cut)
    return factor_of


def gaussian(rng, shape, width, limit, split=(), held_as=jnp.bfloat16):
    loudness = steps_of(rng, shape, split, -0.22, 0.18) if split else 1.0
    entries = jax.random.normal(rng, shape, jnp.float32) * width * loudness
    return jnp.minimum(jnp.maximum(entries, -limit), limit).astype(held_as)


def setup_inputs(seed: int = 0) -> dict:
    keys = jax.random.split(jax.random.key(seed), 14)
    trajectory = gaussian(keys[0], (STEPS, C, NZ, GY, GX), 1.0, 6.0, ((0, 8), (2, 32)))
    noise = gaussian(keys[1], (STEPS, C, NZ, GY, GX), 1.0, 6.0, ((0, 8), (2, 32)))
    start = gaussian(keys[2], (C, NZ, GY, GX), 1.0, 6.0, ((1, 32),), jnp.float32)
    conv_weight = gaussian(keys[3], (27, H, C), (27 * C) ** -0.5, 0.4375)
    conv_bias = gaussian(keys[4], (H,), 0.5, 3.0, (), jnp.float32)
    step_embed = gaussian(keys[5], (STEPS, H), 0.5, 3.0, ((0, 8),), jnp.float32)
    out_weight = gaussian(keys[6], (C, H), (4 * H) ** -0.5, 0.375)
    decoder = gaussian(keys[7], (C,), C ** -0.5, 2.0, (), jnp.float32)
    angle_index = with_ends(jax.random.randint(keys[8], (NV,), 0, ANGLES), jax.random.fold_in(keys[8], 1), 0, ANGLES - 1).astype(jnp.int32)
    measured = gaussian(keys[9], (NS, NV, GX), 1.0, 6.0, ((0, 32),), jnp.float32)
    step_scale = jnp.clip(0.03 + 0.060000004 * jax.random.uniform(keys[10], (STEPS,), jnp.float32) ** steps_of(keys[10], (STEPS,), ((0, 8),), -0.2, 0.2), 0.03, 0.09)
    guide_scale = jnp.clip(jnp.exp(math.log(3.0) - 1.0986123 * jax.random.uniform(keys[11], (STEPS,), jnp.float32) ** steps_of(keys[11], (STEPS,), ((0, 8),), -0.2, 0.2)), 1.0, 3.0)
    noise_scale = jnp.clip(0.05 + 0.15 * jax.random.uniform(keys[12], (STEPS,), jnp.float32) ** steps_of(keys[12], (STEPS,), ((0, 8),), -0.2, 0.2), 0.05, 0.2)
    return {"trajectory": trajectory, "noise": noise, "start": start, "conv_weight": conv_weight, "conv_bias": conv_bias, "step_embed": step_embed, "out_weight": out_weight, "decoder": decoder, "angle_index": angle_index, "measured": measured, "step_scale": step_scale, "guide_scale": guide_scale, "noise_scale": noise_scale}


PROJ = 0.125


def hat_table(angle_index, zpos, ycount, rowcount):
    theta = jnp.pi * angle_index.astype(jnp.float32) / ANGLES
    ypos = jnp.arange(ycount).astype(jnp.float32) - (ycount - 1) / 2.0
    spos = jnp.arange(rowcount).astype(jnp.float32) - (rowcount - 1) / 2.0
    coord = ypos[None, None, :] * jnp.cos(theta)[:, None, None] + zpos[None, :, None] * jnp.sin(theta)[:, None, None]
    table = jnp.maximum(0.0, 1.0 - jnp.abs(coord[None] - spos[:, None, None, None]))
    return table.reshape(rowcount, theta.shape[0], zpos.shape[0] * ycount)


def reference(trajectory, noise, start, conv_weight, conv_bias, step_embed, out_weight, decoder, angle_index, measured, step_scale, guide_scale, noise_scale):
    zpos = jnp.arange(NZ).astype(jnp.float32) - (NZ - 1) / 2.0
    table = hat_table(angle_index, zpos, GY, NS)
    kernel = conv_weight.astype(jnp.float32)
    mixer = out_weight.astype(jnp.float32)

    def one_step(inputs):
        state, step_noise, embed, sscale, gscale, nscale = inputs
        state32 = state.astype(jnp.float32)
        image = jnp.sum(decoder[:, None, None, None] * state32, axis=0)
        sino = PROJ * jnp.einsum("svp,px->svx", table, image.reshape(NZ * GY, GX), precision=lax.Precision.HIGHEST)
        misfit = sino - measured
        back = PROJ * jnp.einsum("svp,svx->px", table, misfit, precision=lax.Precision.HIGHEST)
        back = back.reshape(NZ, GY, GX)
        padded = jnp.pad(state32, ((0, 0), (1, 1), (1, 1), (1, 1)))
        pre = jnp.zeros((H, NZ, GY, GX), jnp.float32)
        for plane_off in range(3):
            for row_off in range(3):
                for col_off in range(3):
                    offset = 9 * plane_off + 3 * row_off + col_off
                    window = padded[:, plane_off:plane_off + NZ, row_off:row_off + GY, col_off:col_off + GX]
                    pre = pre + jnp.einsum("hc,czyx->hzyx", kernel[offset], window)
        pre = pre + conv_bias[:, None, None, None] + embed[:, None, None, None]
        hidden = jax.nn.silu(pre).astype(jnp.bfloat16)
        eps = jnp.einsum("ch,hzyx->czyx", mixer, hidden.astype(jnp.float32))
        guided = eps - gscale * decoder[:, None, None, None] * back[None]
        return sscale * guided + nscale * step_noise.astype(jnp.float32)

    drifts = lax.map(one_step, (trajectory, noise, step_embed, step_scale, guide_scale, noise_scale))
    return start[None] + jnp.cumsum(drifts, axis=0)
```

```python
import functools

import jax
import jax.numpy as jnp
from jax import lax
from jax.experimental import pallas as pl
from jax.experimental.pallas import tpu as pltpu
from jax.sharding import PartitionSpec as P

ANGLES = 180
PROJ = 0.125
NV = 32
NS = 96
WIN = 24
PAD = 168
MSG = 24
F32 = jnp.float32
BF16 = jnp.bfloat16
VMEM = pl.BlockSpec(memory_space=pltpu.VMEM)
SMEM = pl.BlockSpec(memory_space=pltpu.SMEM)


def params(mib):
    return pltpu.CompilerParams(vmem_limit_bytes=mib << 20)


def cost(flops, size, trans=0):
    return pl.CostEstimate(flops=flops, bytes_accessed=size, transcendentals=trans)


def prep_kernel(dec, wk, traj, meas, xp, cum, tot, mm, scr):
    for z in range(4):
        run = None
        for k in range(4):
            acc = None
            for c in range(8):
                v = traj[k, c, z].astype(F32)
                scr[k % 2, c * 32 : (c + 1) * 32, :] = v
                term = dec[c] * v
                acc = term if acc is None else acc + term
            acc = wk[k] * acc
            run = acc if run is None else run + acc
            cum[k, z * 16 : z * 16 + 16, :] = run[:16]
            cum[k, 64 + z * 16 : 64 + z * 16 + 16, :] = run[16:]
            for y in range(0, 32, 2):
                rows = jnp.concatenate(
                    [scr[k % 2, pl.ds(y, 8, stride=32), :], scr[k % 2, pl.ds(y + 1, 8, stride=32), :]], axis=0
                )
                xp[k, z, y * 8 : y * 8 + 16, :] = rows.astype(BF16)
        tot[z * 16 : z * 16 + 16, :] = run[:16]
        tot[64 + z * 16 : 64 + z * 16 + 16, :] = run[16:]
    tot[128:136, :] = jnp.full((8, 128), wk[0] + wk[1] + wk[2] + wk[3], F32)
    mm[...] = jnp.zeros_like(mm)
    for s in range(3):
        x = meas[s]
        tall = jnp.concatenate([x] + [pltpu.roll(x, 128 - 32 * i, 1) for i in range(1, 4)], axis=0)
        mm[pl.ds(s, 32, stride=8), :] = tall.T[:32]


def prep(dec, wk, traj, meas):
    return pl.pallas_call(
        prep_kernel,
        out_shape=(
            jax.ShapeDtypeStruct((4, 4, 256, 128), BF16),
            jax.ShapeDtypeStruct((4, 128, 128), F32),
            jax.ShapeDtypeStruct((136, 128), F32),
            jax.ShapeDtypeStruct((256, 128), F32),
        ),
        in_specs=[SMEM, SMEM, VMEM, VMEM],
        out_specs=(VMEM, VMEM, VMEM, VMEM),
        scratch_shapes=[pltpu.VMEM((2, 256, 128), F32)],
        compiler_params=params(16),
        cost_estimate=cost(4_000_000, 2_600_000),
        name="prep",
    )(dec, wk, traj, meas)


def message_kernel(wk, cum, before, mm, msg, wcol):
    for k in range(4):
        flipped = (cum[k] + before[:128]).T
        for i in range(4):
            msg[pl.ds(4 * i + k, 32, stride=MSG), :] = flipped[32 * i : 32 * i + 32]
    for d in range(32):
        msg[d * MSG + 16 : d * MSG + 24, :] = mm[d * 8 : d * 8 + 8, :]
    sub = lax.broadcasted_iota(jnp.int32, (8, 128), 0) % 4
    w = before[128:136]
    for k in range(4):
        w = w + jnp.where(sub >= k, wk[k], 0.0)
    wcol[...] = w


def message(wk, cum, before, mm):
    return pl.pallas_call(
        message_kernel,
        out_shape=(jax.ShapeDtypeStruct((32 * MSG, 128), F32), jax.ShapeDtypeStruct((8, 128), F32)),
        in_specs=[SMEM, VMEM, VMEM, VMEM],
        out_specs=(VMEM, VMEM),
        compiler_params=params(16),
        cost_estimate=cost(100_000, 900_000),
        name="message",
    )(wk, cum, before, mm)


def conv_kernel(zs, refs_of, ns_in, scale, nscale, *refs):
    ins, rest = refs[:ns_in], refs[ns_in:]
    wt, wo, noise, start = rest[:4]
    extra = rest[4:]
    if len(extra) == 4:
        done, run_ref, tot_ref, scr = extra
    else:
        run_ref, tot_ref, scr = extra
        done = None
    planes = refs_of(ins)
    lane = lax.broadcasted_iota(jnp.int32, (16, 128), 1)
    zero = jnp.zeros((8, 128), BF16)
    for p, plane in enumerate(planes):
        for k in range(4):
            for e in range(3):
                scr[p, e, k, 0:16, :] = jnp.zeros((16, 128), BF16)
                scr[p, e, k, 256:272, :] = jnp.zeros((16, 128), BF16)
            held = zero.astype(F32)
            rows = plane(k)
            for r in range(17):
                if r < 16:
                    cur = rows(r).astype(F32)
                    v = jnp.concatenate([held, cur[:8]], axis=0)
                    held = cur[8:]
                else:
                    v = jnp.concatenate([held, zero.astype(F32)], axis=0)
                left = jnp.where(lane == 0, 0.0, pltpu.roll(v, 1, 1))
                right = jnp.where(lane == 127, 0.0, pltpu.roll(v, 127, 1))
                scr[p, 0, k, r * 16 : r * 16 + 16, :] = left.astype(BF16)
                scr[p, 1, k, r * 16 : r * 16 + 16, :] = v.astype(BF16)
                scr[p, 2, k, r * 16 : r * 16 + 16, :] = right.astype(BF16)
    row = lax.broadcasted_iota(jnp.int32, (16, 256), 0)
    kk = lax.broadcasted_iota(jnp.int32, (16, 256), 1) // 128
    ones = [jnp.where((row < 12) & (row // 3 == kk + 2 * q), 1.0, 0.0).astype(BF16) for q in range(2)]

    def block(step, carry):
        zi, yb = step // 2, step % 2
        first = zi * (1 if zs == (1, 2) else 3)
        zrow = pl.multiple_of(yb * 16, 16)
        acc = [None, None]
        grain = [noise[k, :, zs[0] + zi * (zs[1] - zs[0]), pl.ds(zrow, 16), :].astype(F32) for k in range(4)]
        begin = start[:, zs[0] + zi * (zs[1] - zs[0]), pl.ds(zrow, 16), :]
        for q in range(2):
            for half in range(2):
                hidden = []
                for jj in range(2):
                    top = pl.multiple_of((yb * 4 + half * 2 + jj) * 32, 32)
                    parts = []
                    for e in range(3):
                        for a in range(3):
                            parts.append(
                                jnp.concatenate(
                                    [scr[first + a, e, 2 * q + i, pl.ds(top, 48), :] for i in range(2)], axis=1
                                )
                            )
                    parts.append(ones[q])
                    patch = jnp.concatenate(parts, axis=0)
                    pre = jnp.dot(wt[...], patch, preferred_element_type=F32)
                    hidden.append((pre + pre * jnp.tanh(pre)).astype(BF16))
                eps = jnp.dot(wo[...], jnp.concatenate(hidden, axis=0), preferred_element_type=F32)
                for i in range(2):
                    k = 2 * q + i
                    term = scale[k] * eps[:, i * 128 : i * 128 + 128].reshape(8, 8, 128)
                    term = term + nscale[k] * grain[k][:, half * 8 : half * 8 + 8]
                    acc[half] = term if acc[half] is None else acc[half] + term
                    at = pl.multiple_of(yb * 16 + half * 8, 8)
                    run_ref[k, :, zi, pl.ds(at, 8), :] = acc[half] + begin[:, half * 8 : half * 8 + 8]
        for half in range(2):
            at = pl.multiple_of(yb * 16 + half * 8, 8)
            tot_ref[:, (zs[0] + zi * (zs[1] - zs[0])) if done is not None else zi, pl.ds(at, 8), :] = acc[half]
        return carry

    lax.fori_loop(0, 4, block, 0)
    if done is not None:
        for z in range(2):
            tot_ref[:, 1 + z] = done[:, z]


def conv(zs, planes, scale, nscale, wt, wo, noise, start, done=None):
    inner = zs == (1, 2)

    def refs_of(ins):
        own = ins[0]

        def of(ref, z):
            if z is None:
                return lambda k: (lambda r: ref[k, r * 16 : r * 16 + 16, :])
            return lambda k: (lambda r: ref[k, z, r * 16 : r * 16 + 16, :])

        if inner:
            return [of(own, z) for z in range(4)]
        return [of(ins[1], None), of(own, 0), of(own, 1), of(own, 2), of(own, 3), of(ins[2], None)]

    more = [] if done is None else [done]
    depth = 2 if done is None else 4
    return pl.pallas_call(
        functools.partial(conv_kernel, zs, refs_of, len(planes)),
        out_shape=(
            jax.ShapeDtypeStruct((4, 8, 2, 32, 128), F32),
            jax.ShapeDtypeStruct((8, depth, 32, 128), F32),
        ),
        in_specs=[SMEM, SMEM] + [VMEM] * (len(planes) + 4 + len(more)),
        out_specs=(VMEM, VMEM),
        scratch_shapes=[pltpu.VMEM((4 if inner else 6, 3, 4, 272, 128), BF16)],
        compiler_params=params(40),
        cost_estimate=cost(6_000_000_000, 4_000_000, 2_000_000),
        name="conv_inner" if inner else "conv_outer",
    )(scale, nscale, *planes, wt, wo, noise, start, *more)


def project_kernel(base, off, cosv, sinv, wcol, got, out, table, sino, meas):
    lane = lax.broadcasted_iota(jnp.int32, (16, 128), 1)
    low = lane < 64
    sino[...] = jnp.zeros_like(sino)
    for d in range(32):
        meas[3 * d : 3 * d + 3, :] = got[d * MSG + 16 : d * MSG + 19, :]
    cell = lax.broadcasted_iota(jnp.int32, (8, 256), 1)
    dy = (cell % 16).astype(F32)
    dz = (cell // 16).astype(F32)
    sub = lax.broadcasted_iota(jnp.int32, (8, 256), 0).astype(F32)

    def where_rows(t, v):
        return v * PAD + 24 + base[t * NV + v]

    def forward(zt, carry):
        slab = [got[pl.ds(pl.multiple_of((4 * zt + i) * MSG, 8), 16), :] for i in range(4)]
        flip = [pltpu.roll(s, 64, 1) for s in slab]
        tiles = [
            jnp.concatenate([jnp.where(low, slab[0], flip[1]), jnp.where(low, slab[2], flip[3])], axis=1),
            jnp.concatenate([jnp.where(low, flip[0], slab[1]), jnp.where(low, flip[2], slab[3])], axis=1),
        ]
        for yt in range(2):
            t = zt * 2 + yt
            image = tiles[yt]
            hi = image.astype(BF16)
            lo = (image - hi.astype(F32)).astype(BF16)
            gap = jnp.zeros((16, 256), BF16)
            columns = jnp.concatenate([gap, gap, hi, gap, lo, gap, gap, gap], axis=0)
            columns = jnp.concatenate([columns, columns], axis=1)
            for v in range(0, NV, 2):
                rows = []
                for u in (v, v + 1):
                    at = dy * cosv[u] + dz * sinv[u] + off[t * NV + u]
                    for b in range(3):
                        rows.append(jnp.maximum(0.0, 1.0 - jnp.abs(at - (sub + 8.0 * b))))
                hat = jnp.concatenate(rows, axis=0)
                top = hat.astype(BF16)
                rest = (hat - top.astype(F32)).astype(BF16)
                table[t, v * WIN : (v + 2) * WIN, 0:256] = top
                table[t, v * WIN : (v + 2) * WIN, 256:512] = rest
            sums = lax.dot_general(table[t], columns, (((1,), (1,)), ((), ())), preferred_element_type=F32)
            for v in range(NV):
                at = pl.ds(where_rows(t, v), WIN)
                sino[at, :] = sino[at, :] + sums[v * WIN : (v + 1) * WIN]
        return carry

    lax.fori_loop(0, 8, forward, 0)

    wide = lax.broadcasted_iota(jnp.int32, (NS, 128), 1)

    def misfit(v, carry):
        at = pl.multiple_of(v * PAD, 8)
        rows = sino[pl.ds(at + 24, NS), :]
        rows = PROJ * (rows + pltpu.roll(rows, 96, 1))
        hi = rows.astype(BF16).astype(F32)
        lo = pltpu.roll(rows - hi, 32, 1)
        seen = pltpu.roll(meas[...], lax.rem(128 + 24 - v, 128), 1)
        seen_hi = seen.astype(BF16).astype(F32)
        seen_lo = pltpu.roll(seen - seen_hi, 1, 1)
        spread = jnp.where(
            (wide >= 32) & (wide < 48),
            hi,
            jnp.where(
                (wide >= 64) & (wide < 80),
                lo,
                jnp.where(wide % 32 == 24, seen_hi, jnp.where(wide % 32 == 25, seen_lo, 0.0)),
            ),
        )
        sino[pl.ds(at, 24), :] = jnp.zeros((24, 128), F32)
        sino[pl.ds(at + 24, NS), :] = spread
        sino[pl.ds(at + 120, 48), :] = jnp.zeros((48, 128), F32)
        return carry

    lax.fori_loop(0, NV, misfit, 0)

    upper = lax.broadcasted_iota(jnp.int32, (8, 256), 0) < 4
    wk = jnp.concatenate([wcol[...], wcol[...]], axis=1)

    def backward(zt, carry):
        tiles = []
        for yt in range(2):
            t = zt * 2 + yt
            rows = jnp.concatenate([sino[pl.ds(where_rows(t, v), WIN), :] for v in range(NV)], axis=0)
            sums = lax.dot_general(
                rows.astype(BF16), table[t], (((0,), (0,)), ((), ())), preferred_element_type=F32
            )
            sums = sums[:, :256] + sums[:, 256:]
            pair = []
            for h in range(2):
                seen = [
                    sums[24 + 32 * i : 25 + 32 * i] + sums[25 + 32 * i : 26 + 32 * i] for i in (2 * h, 2 * h + 1)
                ]
                ours = sums[32 + 8 * h : 40 + 8 * h] + sums[64 + 8 * h : 72 + 8 * h]
                pair.append(PROJ * (ours - wk * jnp.where(upper, seen[0], seen[1])))
            tiles.append(jnp.concatenate(pair, axis=0))
        for h in range(2):
            a, b = (tile[:, 128 * h : 128 * h + 128] for tile in tiles)
            at = pl.multiple_of((4 * zt + 2 * h) * 16, 16)
            out[pl.ds(at, 16), :] = jnp.where(low, a, pltpu.roll(b, 64, 1))
            out[pl.ds(at + 16, 16), :] = jnp.where(low, pltpu.roll(a, 64, 1), b)
        return carry

    lax.fori_loop(0, 8, backward, 0)


def project(base, off, cosv, sinv, wcol, got):
    return pl.pallas_call(
        project_kernel,
        out_shape=jax.ShapeDtypeStruct((512, 128), F32),
        in_specs=[SMEM, SMEM, SMEM, SMEM, VMEM, VMEM],
        out_specs=VMEM,
        scratch_shapes=[
            pltpu.VMEM((16, NV * WIN, 512), BF16),
            pltpu.VMEM((NV * PAD, 128), F32),
            pltpu.VMEM((NS, 128), F32),
        ],
        compiler_params=params(40),
        cost_estimate=cost(8_000_000_000, 2_000_000),
        name="project",
    )(base, off, cosv, sinv, wcol, got)


def final_kernel(dec, back, inner, outer, before, new):
    k = pl.program_id(0)
    columns = jnp.concatenate([back[pl.ds(4 * i + k, 32, stride=16), :] for i in range(4)], axis=0)
    cells = columns.T
    for z in range(4):
        guide = jnp.concatenate([cells[z * 16 : z * 16 + 16], cells[64 + z * 16 : 80 + z * 16]], axis=0)
        own = inner[0, :, z - 1] if z in (1, 2) else outer[0, :, z // 3]
        for c in range(8):
            new[0, c, z] = own[c] + before[c, z] - dec[c] * guide


def final(dec, back, inner, outer, before):
    whole = pl.BlockSpec((512, 128), lambda k: (0, 0))
    part = pl.BlockSpec((1, 8, 2, 32, 128), lambda k: (k, 0, 0, 0, 0))
    return pl.pallas_call(
        final_kernel,
        grid=(4,),
        out_shape=jax.ShapeDtypeStruct((4, 8, 4, 32, 128), F32),
        in_specs=[SMEM, whole, part, part, pl.BlockSpec((8, 4, 32, 128), lambda k: (0, 0, 0, 0))],
        out_specs=pl.BlockSpec((1, 8, 4, 32, 128), lambda k: (k, 0, 0, 0, 0)),
        compiler_params=params(24),
        cost_estimate=cost(2_000_000, 5_000_000),
        name="final",
    )(dec, back, inner, outer, before)


def shifted(value, axis, step):
    count = lax.axis_size(axis)
    return lax.ppermute(value, axis, [(i, i + step) for i in range(count) if 0 <= i + step < count])


def earlier(value):
    odd = (lax.axis_index("tm") % 2).astype(F32)
    other = lax.ppermute(value, "tm", [(i, i ^ 1) for i in range(lax.axis_size("tm"))])
    total = value + other
    before = odd * other
    near = shifted(total, "tm", 2)
    far = shifted(total + near, "tm", 4)
    return before + near + far


def conv_tables(conv_weight, conv_bias, step_embed, out_weight):
    w = (conv_weight.astype(F32) * 0.5).reshape(3, 3, 3, 64, 8)
    w = w.transpose(3, 2, 0, 1, 4)
    rows = [jnp.pad(w, ((0, 0), (0, 0), (0, 0), (o, 3 - o), (0, 0))).reshape(64, 432) for o in range(4)]
    bias = 0.5 * (conv_bias[None] + step_embed)
    hi = lax.reduce_precision(bias, 8, 7)
    mid = lax.reduce_precision(bias - hi, 8, 7)
    low = bias - hi - mid
    extra = jnp.stack([hi, mid, low], axis=1).reshape(12, 64).T
    extra = jnp.pad(extra, ((0, 0), (0, 4)))
    wt = jnp.concatenate([jnp.concatenate([r, extra], axis=1) for r in rows], axis=0).astype(BF16)
    wo = out_weight[:, None, None, :] * jnp.eye(8, dtype=BF16)[None, :, :, None]
    return wt, wo.reshape(64, 512)


def windows(angle_index):
    theta = jnp.pi * angle_index.astype(F32) / ANGLES
    cosv, sinv = jnp.cos(theta), jnp.sin(theta)
    tile = jnp.arange(16)
    z0 = (16 * (tile // 2)).astype(F32) - 63.5
    y0 = (16 * (tile % 2)).astype(F32) - 15.5
    corner = y0[:, None] * cosv[None] + z0[:, None] * sinv[None] + 47.5
    least = corner + jnp.minimum(0.0, 15.0 * cosv)[None] + jnp.minimum(0.0, 15.0 * sinv)[None]
    base = jnp.floor(least - 0.001)
    return base.astype(jnp.int32).reshape(512), (corner - base).reshape(512), cosv, sinv


def on_device(
    trajectory,
    noise,
    start,
    conv_weight,
    conv_bias,
    step_embed,
    out_weight,
    decoder,
    angle_index,
    measured,
    step_scale,
    guide_scale,
    noise_scale,
):
    weight = step_scale * guide_scale
    xp, cum, tot, mm = prep(decoder, weight, trajectory, measured)
    up = shifted(xp[:, 3], "space", 1)
    down = shifted(xp[:, 0], "space", -1)
    before_image = earlier(tot)
    wt, wo = conv_tables(conv_weight, conv_bias, step_embed, out_weight)
    base, off, cosv, sinv = windows(angle_index)
    inner, part = conv((1, 2), [xp], step_scale, noise_scale, wt, wo, noise, start)
    outer, own = conv((0, 3), [xp, up, down], step_scale, noise_scale, wt, wo, noise, start, part)
    before = earlier(own)
    msg, wcol = message(weight, cum, before_image, mm)
    got = lax.all_to_all(msg.reshape(32, MSG, 128), "space", 0, 0, tiled=True)
    back = project(base, off, cosv, sinv, wcol, got.reshape(32 * MSG, 128))
    back = lax.all_to_all(back.reshape(32, 16, 128), "space", 0, 0, tiled=True)
    return final(decoder, back.reshape(512, 128), inner, outer, before)


def solution(mesh):
    return jax.shard_map(
        on_device,
        mesh=mesh,
        in_specs=(
            P("tm", None, "space", None, None),
            P("tm", None, "space", None, None),
            P(None, "space", None, None),
            P(),
            P(),
            P("tm", None),
            P(),
            P(),
            P(),
            P("space", None, None),
            P("tm"),
            P("tm"),
            P("tm"),
        ),
        out_specs=P("tm", None, "space", None, None),
        check_vma=False,
    )
```

```python
import functools

import jax
import jax.numpy as jnp
from jax import lax
from jax.experimental import pallas as pl
from jax.experimental.pallas import tpu as pltpu
from jax.sharding import PartitionSpec as P

ANGLES = 180
PROJ = 0.125
NV = 32
NS = 96
WIN = 24
PAD = 168
MSG = 24
F32 = jnp.float32
BF16 = jnp.bfloat16
VMEM = pl.BlockSpec(memory_space=pltpu.VMEM)
SMEM = pl.BlockSpec(memory_space=pltpu.SMEM)
ANY = pl.BlockSpec(memory_space=pl.ANY)
HBM = pl.BlockSpec(memory_space=pltpu.HBM)


def params(mib):
    return pltpu.CompilerParams(vmem_limit_bytes=mib << 20)


def in_hbm(*values):
    return [pltpu.with_memory_space_constraint(v, pltpu.HBM) for v in values]


def cost(flops, size, trans=0):
    return pl.CostEstimate(flops=flops, bytes_accessed=size, transcendentals=trans)


def prep_kernel(
    dec_from, scale_from, guide_from, source, meas_from, xp, top, bottom, cum, tot, mm, dec, scale, guide, meas, traj, sems, scr
):
    small = [(dec_from, dec), (scale_from, scale), (guide_from, guide), (meas_from, meas)]
    small = [pltpu.make_async_copy(a, b, sems.at[4 + i]) for i, (a, b) in enumerate(small)]
    copies = [pltpu.make_async_copy(source.at[:, :, z], traj.at[z], sems.at[z]) for z in range(4)]
    for copy in small + copies:
        copy.start()
    for copy in small:
        copy.wait()
    wk = [scale[k] * guide[k] for k in range(4)]
    mm[...] = jnp.zeros_like(mm)
    for s in range(3):
        x = meas[s]
        tall = jnp.concatenate([x] + [pltpu.roll(x, 128 - 32 * i, 1) for i in range(1, 4)], axis=0)
        mm[pl.ds(s, 32, stride=8), :] = tall.T[:32]
    for z in range(4):
        copies[z].wait()
        run = None
        for k in range(4):
            acc = None
            for c in range(8):
                v = traj[z, k, c].astype(F32)
                scr[k % 2, c * 32 : (c + 1) * 32, :] = v
                term = dec[c] * v
                acc = term if acc is None else acc + term
            acc = wk[k] * acc
            run = acc if run is None else run + acc
            cum[k, z * 16 : z * 16 + 16, :] = run[:16]
            cum[k, 64 + z * 16 : 64 + z * 16 + 16, :] = run[16:]
            for y in range(0, 32, 2):
                rows = jnp.concatenate(
                    [scr[k % 2, pl.ds(y, 8, stride=32), :], scr[k % 2, pl.ds(y + 1, 8, stride=32), :]], axis=0
                )
                rows = rows.astype(BF16)
                xp[k, z, y * 8 : y * 8 + 16, :] = rows
                if z == 0:
                    bottom[k, y * 8 : y * 8 + 16, :] = rows
                if z == 3:
                    top[k, y * 8 : y * 8 + 16, :] = rows
        tot[z * 16 : z * 16 + 16, :] = run[:16]
        tot[64 + z * 16 : 64 + z * 16 + 16, :] = run[16:]
    tot[128:136, :] = jnp.full((8, 128), wk[0] + wk[1] + wk[2] + wk[3], F32)


def prep(dec, scale, guide, traj, meas):
    return pl.pallas_call(
        prep_kernel,
        out_shape=(
            jax.ShapeDtypeStruct((4, 4, 256, 128), BF16),
            jax.ShapeDtypeStruct((4, 256, 128), BF16),
            jax.ShapeDtypeStruct((4, 256, 128), BF16),
            jax.ShapeDtypeStruct((4, 128, 128), F32),
            jax.ShapeDtypeStruct((136, 128), F32),
            jax.ShapeDtypeStruct((256, 128), F32),
        ),
        in_specs=[HBM] * 5,
        out_specs=(VMEM,) * 6,
        scratch_shapes=[
            pltpu.SMEM((8,), F32),
            pltpu.SMEM((4,), F32),
            pltpu.SMEM((4,), F32),
            pltpu.VMEM((3, 32, 128), F32),
            pltpu.VMEM((4, 4, 8, 32, 128), BF16),
            pltpu.SemaphoreType.DMA((8,)),
            pltpu.VMEM((2, 256, 128), F32),
        ],
        compiler_params=params(16),
        cost_estimate=cost(4_000_000, 2_600_000),
        name="prep",
    )(*in_hbm(dec, scale, guide, traj, meas))


def message_kernel(scale, guide, odd, cum, other, one, two, three, mm, held, msg, passed):
    wk = [scale[k] * guide[k] for k in range(4)]
    before = jnp.where(odd[0] == 0, 0.0, other[...]) + (one[...] + two[...] + three[...])
    for k in range(4):
        flipped = (cum[k] + before[:128]).T
        for i in range(4):
            msg[pl.ds(4 * i + k, 32, stride=MSG), :] = flipped[32 * i : 32 * i + 32]
    sub = lax.broadcasted_iota(jnp.int32, (8, 128), 0)
    w = before[128:136]
    for k in range(4):
        w = w + jnp.where(sub % 4 >= k, wk[k], 0.0)
    for d in range(32):
        msg[d * MSG + 16 : d * MSG + 24, :] = jnp.where(sub >= 4, w, mm[d * 8 : d * 8 + 8, :])


def message(scale, guide, odd, cum, parts, mm, held):
    return pl.pallas_call(
        message_kernel,
        out_shape=(
            jax.ShapeDtypeStruct((32 * MSG, 128), F32),
            jax.ShapeDtypeStruct(held.shape, held.dtype),
        ),
        in_specs=[SMEM, SMEM, SMEM] + [VMEM] * 6 + [ANY],
        out_specs=(VMEM, ANY),
        input_output_aliases={9: 1},
        compiler_params=params(8),
        cost_estimate=cost(100_000, 900_000),
        name="message",
    )(scale, guide, odd, cum, *parts, mm, held)


def conv_kernel(zs, refs_of, ns_in, scale, nscale, *refs):
    ins, rest = list(refs[:ns_in]), refs[ns_in:]
    wt, wo, noise_from, start_from = rest[:4]
    extra = rest[4:]
    done = None
    fetched = {}
    if ns_in == 3:
        done_from, odd, extra = extra[0], extra[1], extra[2:]
        run_ref, tot_ref, give_ref, scr, noise, start, sems, held_planes, done, more_sems = extra
        sources = [ins[1], ins[0].at[:, 0], ins[0].at[:, 1], ins[0].at[:, 2], ins[0].at[:, 3], ins[2]]
        for p, source in enumerate(sources):
            fetched[p] = pltpu.make_async_copy(source, held_planes.at[p], more_sems.at[p])
            fetched[p].start()
        fetched[6] = pltpu.make_async_copy(done_from, done, more_sems.at[6])
        fetched[6].start()
        ins = [held_planes]
    else:
        run_ref, tot_ref, scr, noise, start, sems = extra

    def put(value, z, rows):
        if done is None:
            tot_ref[:, z, rows, :] = value
        else:
            low, high = value[:4], value[4:]
            tot_ref[:, z, rows, :] = jnp.where(odd[0] == 0, low, high)
            give_ref[:, z, rows, :] = jnp.where(odd[0] == 0, high, low)

    copies = []
    for i, z in enumerate(zs):
        copies.append(pltpu.make_async_copy(noise_from.at[:, :, z], noise.at[i], sems.at[0, i]))
        copies.append(pltpu.make_async_copy(start_from.at[:, z], start.at[i], sems.at[1, i]))
    for copy in copies:
        copy.start()
    planes = refs_of(ins)
    lane = lax.broadcasted_iota(jnp.int32, (16, 128), 1)
    zero = jnp.zeros((8, 128), BF16)
    for p, plane in enumerate(planes):
        if fetched:
            fetched[p].wait()
        for k in range(4):
            for e in range(3):
                scr[p, e, k, 0:16, :] = jnp.zeros((16, 128), BF16)
                scr[p, e, k, 256:272, :] = jnp.zeros((16, 128), BF16)
            held = zero.astype(F32)
            rows = plane(k)
            for r in range(17):
                if r < 16:
                    cur = rows(r).astype(F32)
                    v = jnp.concatenate([held, cur[:8]], axis=0)
                    held = cur[8:]
                else:
                    v = jnp.concatenate([held, zero.astype(F32)], axis=0)
                left = jnp.where(lane == 0, 0.0, pltpu.roll(v, 1, 1))
                right = jnp.where(lane == 127, 0.0, pltpu.roll(v, 127, 1))
                scr[p, 0, k, r * 16 : r * 16 + 16, :] = left.astype(BF16)
                scr[p, 1, k, r * 16 : r * 16 + 16, :] = v.astype(BF16)
                scr[p, 2, k, r * 16 : r * 16 + 16, :] = right.astype(BF16)
    row = lax.broadcasted_iota(jnp.int32, (16, 512), 0)
    kk = lax.broadcasted_iota(jnp.int32, (16, 512), 1) // 128
    ones = jnp.where((row < 12) & (row // 3 == kk), 1.0, 0.0).astype(BF16)

    for copy in copies:
        copy.wait()

    def block(step, carry):
        zi, yb = step // 2, step % 2
        first = zi * (1 if zs == (1, 2) else 3)
        zrow = pl.multiple_of(yb * 16, 16)
        grain = [noise[zi, k, :, pl.ds(zrow, 16), :].astype(F32) for k in range(4)]
        begin = start[zi, :, pl.ds(zrow, 16), :]
        for half in range(2):
            hidden = []
            for jj in range(2):
                top = pl.multiple_of((yb * 4 + half * 2 + jj) * 32, 32)
                parts = []
                for e in range(3):
                    for a in range(3):
                        parts.append(
                            jnp.concatenate([scr[first + a, e, k, pl.ds(top, 48), :] for k in range(4)], axis=1)
                        )
                parts.append(ones)
                patch = jnp.concatenate(parts, axis=0)
                pre = jnp.dot(wt[...], patch, preferred_element_type=F32)
                hidden.append((pre + pre * jnp.tanh(pre)).astype(BF16))
            eps = jnp.dot(wo[...], jnp.concatenate(hidden, axis=0), preferred_element_type=F32)
            at = pl.multiple_of(yb * 16 + half * 8, 8)
            acc = None
            for k in range(4):
                term = scale[k] * eps[:, k * 128 : k * 128 + 128].reshape(8, 8, 128)
                term = term + nscale[k] * grain[k][:, half * 8 : half * 8 + 8]
                acc = term if acc is None else acc + term
                run_ref[k, :, zi, pl.ds(at, 8), :] = acc + begin[:, half * 8 : half * 8 + 8]
            put(acc, zi if done is None else 3 * zi, pl.ds(at, 8))
        return carry

    lax.fori_loop(0, 4, block, 0)
    if done is not None:
        fetched[6].wait()
        for z in range(2):
            put(done[:, z], 1 + z, pl.ds(0, 32))


def conv(zs, planes, scale, nscale, wt, wo, noise, start, done=None, odd=None):
    inner = zs == (1, 2)

    def refs_of(ins):
        own = ins[0]

        def of(z):
            if inner:
                return lambda k: (lambda r: own[k, z, r * 16 : r * 16 + 16, :])
            return lambda k: (lambda r: own[z, k, r * 16 : r * 16 + 16, :])

        return [of(z) for z in range(4 if inner else 6)]

    more = [] if done is None else [*in_hbm(done), odd]
    extra = []
    if not inner:
        planes = in_hbm(*planes)
        extra = [
            pltpu.VMEM((6, 4, 256, 128), BF16),
            pltpu.VMEM((8, 2, 32, 128), F32),
            pltpu.SemaphoreType.DMA((7,)),
        ]
    sums = [jax.ShapeDtypeStruct((8, 2, 32, 128), F32)]
    if done is not None:
        sums = [jax.ShapeDtypeStruct((4, 4, 32, 128), F32)] * 2
    return pl.pallas_call(
        functools.partial(conv_kernel, zs, refs_of, len(planes)),
        out_shape=(
            jax.ShapeDtypeStruct((4, 8, 2, 32, 128), F32),
            *sums,
        ),
        in_specs=[SMEM, SMEM]
        + [VMEM if inner else HBM] * len(planes)
        + [VMEM, VMEM, HBM, HBM]
        + [HBM, SMEM][: len(more)],
        out_specs=(VMEM,) * (1 + len(sums)),
        scratch_shapes=[
            pltpu.VMEM((4 if inner else 6, 3, 4, 272, 128), BF16),
            pltpu.VMEM((2, 4, 8, 32, 128), BF16),
            pltpu.VMEM((2, 8, 32, 128), F32),
            pltpu.SemaphoreType.DMA((2, 2)),
            *extra,
        ],
        compiler_params=params(16),
        cost_estimate=cost(6_000_000_000, 4_000_000, 2_000_000),
        name="conv_inner" if inner else "conv_outer",
    )(scale, nscale, *planes, wt, wo, *in_hbm(noise, start), *more)


def project_kernel(base, off, cosv, sinv, got, out, table, sino, meas):
    lane = lax.broadcasted_iota(jnp.int32, (16, 128), 1)
    low = lane < 64
    sino[...] = jnp.zeros_like(sino)
    for d in range(32):
        meas[3 * d : 3 * d + 3, :] = got[d * MSG + 16 : d * MSG + 19, :]
    cell = lax.broadcasted_iota(jnp.int32, (8, 256), 1)
    dy = (cell % 16).astype(F32)
    dz = (cell // 16).astype(F32)
    sub = lax.broadcasted_iota(jnp.int32, (8, 256), 0).astype(F32)

    def where_rows(t, v):
        return v * PAD + 24 + base[t * NV + v]

    def forward(zt, carry):
        slab = [got[pl.ds(pl.multiple_of((4 * zt + i) * MSG, 8), 16), :] for i in range(4)]
        flip = [pltpu.roll(s, 64, 1) for s in slab]
        tiles = [
            jnp.concatenate([jnp.where(low, slab[0], flip[1]), jnp.where(low, slab[2], flip[3])], axis=1),
            jnp.concatenate([jnp.where(low, flip[0], slab[1]), jnp.where(low, flip[2], slab[3])], axis=1),
        ]
        for yt in range(2):
            t = zt * 2 + yt
            image = tiles[yt]
            hi = image.astype(BF16)
            lo = (image - hi.astype(F32)).astype(BF16)
            gap = jnp.zeros((16, 256), BF16)
            columns = jnp.concatenate([gap, gap, hi, gap, lo, gap, gap, gap], axis=0)
            columns = jnp.concatenate([columns, columns], axis=1)
            for v in range(0, NV, 2):
                rows = []
                for u in (v, v + 1):
                    at = dy * cosv[u] + dz * sinv[u] + off[t * NV + u]
                    for b in range(3):
                        rows.append(jnp.maximum(0.0, 1.0 - jnp.abs(at - (sub + 8.0 * b))))
                hat = jnp.concatenate(rows, axis=0)
                top = hat.astype(BF16)
                rest = (hat - top.astype(F32)).astype(BF16)
                table[t, v * WIN : (v + 2) * WIN, 0:256] = top
                table[t, v * WIN : (v + 2) * WIN, 256:512] = rest
            sums = lax.dot_general(table[t], columns, (((1,), (1,)), ((), ())), preferred_element_type=F32)
            for v in range(NV):
                at = pl.ds(where_rows(t, v), WIN)
                sino[at, :] = sino[at, :] + sums[v * WIN : (v + 1) * WIN]
        return carry

    lax.fori_loop(0, 8, forward, 0)

    wide = lax.broadcasted_iota(jnp.int32, (NS, 128), 1)

    def misfit(v):
        at = pl.multiple_of(v * PAD, 8)
        rows = sino[pl.ds(at + 24, NS), :]
        rows = PROJ * (rows + pltpu.roll(rows, 96, 1))
        hi = rows.astype(BF16).astype(F32)
        lo = pltpu.roll(rows - hi, 32, 1)
        seen = pltpu.roll(meas[...], lax.rem(128 + 24 - v, 128), 1)
        seen_hi = seen.astype(BF16).astype(F32)
        seen_lo = pltpu.roll(seen - seen_hi, 1, 1)
        spread = jnp.where(
            (wide >= 32) & (wide < 48),
            hi,
            jnp.where(
                (wide >= 64) & (wide < 80),
                lo,
                jnp.where(wide % 32 == 24, seen_hi, jnp.where(wide % 32 == 25, seen_lo, 0.0)),
            ),
        )
        sino[pl.ds(at, 24), :] = jnp.zeros((24, 128), F32)
        sino[pl.ds(at + 24, NS), :] = spread
        sino[pl.ds(at + 120, 48), :] = jnp.zeros((48, 128), F32)

    def misfits(group, carry):
        for v in range(4):
            misfit(group * 4 + v)
        return carry

    lax.fori_loop(0, NV // 4, misfits, 0)

    upper = lax.broadcasted_iota(jnp.int32, (8, 256), 0) < 4
    wk = got[16:24, :]
    wk = jnp.where(upper[:, :128], pltpu.roll(wk, 4, 0), wk)
    wk = jnp.concatenate([wk, wk], axis=1)

    def backward(zt, carry):
        tiles = []
        for yt in range(2):
            t = zt * 2 + yt
            rows = jnp.concatenate([sino[pl.ds(where_rows(t, v), WIN), :] for v in range(NV)], axis=0)
            sums = lax.dot_general(
                rows.astype(BF16), table[t], (((0,), (0,)), ((), ())), preferred_element_type=F32
            )
            sums = sums[:, :256] + sums[:, 256:]
            pair = []
            for h in range(2):
                seen = [
                    sums[24 + 32 * i : 25 + 32 * i] + sums[25 + 32 * i : 26 + 32 * i] for i in (2 * h, 2 * h + 1)
                ]
                ours = sums[32 + 8 * h : 40 + 8 * h] + sums[64 + 8 * h : 72 + 8 * h]
                pair.append(PROJ * (ours - wk * jnp.where(upper, seen[0], seen[1])))
            tiles.append(jnp.concatenate(pair, axis=0))
        for h in range(2):
            a, b = (tile[:, 128 * h : 128 * h + 128] for tile in tiles)
            at = pl.multiple_of((4 * zt + 2 * h) * 16, 16)
            out[pl.ds(at, 16), :] = jnp.where(low, a, pltpu.roll(b, 64, 1))
            out[pl.ds(at + 16, 16), :] = jnp.where(low, pltpu.roll(a, 64, 1), b)
        return carry

    lax.fori_loop(0, 8, backward, 0)


def project(base, off, cosv, sinv, got):
    return pl.pallas_call(
        project_kernel,
        out_shape=jax.ShapeDtypeStruct((512, 128), F32),
        in_specs=[SMEM, SMEM, SMEM, SMEM, VMEM],
        out_specs=VMEM,
        scratch_shapes=[
            pltpu.VMEM((16, NV * WIN, 512), BF16),
            pltpu.VMEM((NV * PAD, 128), F32),
            pltpu.VMEM((NS, 128), F32),
        ],
        compiler_params=params(22),
        cost_estimate=cost(8_000_000_000, 2_000_000),
        name="project",
    )(base, off, cosv, sinv, got)


def final_kernel(dec, odd, back, inner, outer, mine, theirs, new):
    k = pl.program_id(0)
    columns = jnp.concatenate([back[pl.ds(4 * i + k, 32, stride=16), :] for i in range(4)], axis=0)
    cells = columns.T
    for z in range(4):
        guide = jnp.concatenate([cells[z * 16 : z * 16 + 16], cells[64 + z * 16 : 80 + z * 16]], axis=0)
        for c in range(8):
            own = inner[0, c, z - 1] if z in (1, 2) else outer[0, c, z // 3]
            before = jnp.where(odd[0] == c // 4, mine[c % 4, z], theirs[c % 4, z])
            new[0, c, z] = own + before - dec[c] * guide


def final(dec, odd, back, inner, outer, mine, theirs):
    whole = pl.BlockSpec((512, 128), lambda k: (0, 0))
    part = pl.BlockSpec((1, 8, 2, 32, 128), lambda k: (k, 0, 0, 0, 0))
    half = pl.BlockSpec((4, 4, 32, 128), lambda k: (0, 0, 0, 0))
    return pl.pallas_call(
        final_kernel,
        grid=(4,),
        out_shape=jax.ShapeDtypeStruct((4, 8, 4, 32, 128), F32),
        in_specs=[SMEM, SMEM, whole, part, part, half, half],
        out_specs=pl.BlockSpec((1, 8, 4, 32, 128), lambda k: (k, 0, 0, 0, 0)),
        compiler_params=params(16),
        cost_estimate=cost(2_000_000, 5_000_000),
        name="final",
    )(*in_hbm(dec), odd, back, inner, outer, mine, theirs)


def add_kernel(a, b, held, out, passed):
    out[...] = a[...] + b[...]


def add_then(a, b, held):
    return pl.pallas_call(
        add_kernel,
        out_shape=(jax.ShapeDtypeStruct(a.shape, F32), jax.ShapeDtypeStruct(held.shape, held.dtype)),
        in_specs=[VMEM, VMEM, ANY],
        out_specs=(VMEM, ANY),
        input_output_aliases={2: 1},
        compiler_params=params(4),
        cost_estimate=cost(100_000, 800_000),
        name="add_then",
    )(a, b, held)


def send_kernel(odd, near, far, keep, given, held, send, mine, passed):
    first = odd[0] == 0
    chips = near[...] + far[...]
    send[...] = chips + jnp.where(first, keep[...], 0.0)
    mine[...] = chips + jnp.where(first, 0.0, given[...])


def send_then(odd, near, far, keep, given, held):
    return pl.pallas_call(
        send_kernel,
        out_shape=(jax.ShapeDtypeStruct(near.shape, F32),) * 2 + (jax.ShapeDtypeStruct(held.shape, held.dtype),),
        in_specs=[SMEM, VMEM, VMEM, VMEM, VMEM, ANY],
        out_specs=(VMEM, VMEM, ANY),
        input_output_aliases={5: 2},
        compiler_params=params(4),
        cost_estimate=cost(100_000, 1_500_000),
        name="send_then",
    )(odd, near, far, keep, given, held)


def shifted(value, axis, step):
    count = lax.axis_size(axis)
    return lax.ppermute(value, axis, [(i, i + step) for i in range(count) if 0 <= i + step < count])


def other_core(value):
    return lax.ppermute(value, "tm", [(i, i ^ 1) for i in range(lax.axis_size("tm"))])


def conv_tables(conv_weight, conv_bias, step_embed, out_weight):
    w = (conv_weight.astype(F32) * 0.5).reshape(3, 3, 3, 64, 8)
    w = w.transpose(3, 2, 0, 1, 4)
    rows = [jnp.pad(w, ((0, 0), (0, 0), (0, 0), (o, 3 - o), (0, 0))).reshape(64, 432) for o in range(4)]
    bias = 0.5 * (conv_bias[None] + step_embed)
    hi = lax.reduce_precision(bias, 8, 7)
    mid = lax.reduce_precision(bias - hi, 8, 7)
    low = bias - hi - mid
    extra = jnp.stack([hi, mid, low], axis=1).reshape(12, 64).T
    extra = jnp.pad(extra, ((0, 0), (0, 4)))
    wt = jnp.concatenate([jnp.concatenate([r, extra], axis=1) for r in rows], axis=0).astype(BF16)
    wo = out_weight[:, None, None, :] * jnp.eye(8, dtype=BF16)[None, :, :, None]
    return wt, wo.reshape(64, 512)


def windows(angle_index):
    theta = jnp.pi * angle_index.astype(F32) / ANGLES
    cosv, sinv = jnp.cos(theta), jnp.sin(theta)
    tile = jnp.arange(16)
    z0 = (16 * (tile // 2)).astype(F32) - 63.5
    y0 = (16 * (tile % 2)).astype(F32) - 15.5
    corner = y0[:, None] * cosv[None] + z0[:, None] * sinv[None] + 47.5
    least = corner + jnp.minimum(0.0, 15.0 * cosv)[None] + jnp.minimum(0.0, 15.0 * sinv)[None]
    base = jnp.floor(least - 0.001)
    return base.astype(jnp.int32).reshape(512), (corner - base).reshape(512), cosv, sinv


def on_device(
    trajectory,
    noise,
    start,
    conv_weight,
    conv_bias,
    step_embed,
    out_weight,
    decoder,
    angle_index,
    measured,
    step_scale,
    guide_scale,
    noise_scale,
):
    odd = (lax.axis_index("tm") % 2).reshape(1)
    xp, top, bottom, cum, tot, mm = prep(decoder, step_scale, guide_scale, trajectory, measured)
    up = shifted(top, "space", 1)
    down = shifted(bottom, "space", -1)
    other = other_core(tot)
    wt, wo = conv_tables(conv_weight, conv_bias, step_embed, out_weight)
    base, off, cosv, sinv = windows(angle_index)
    inner, part = conv((1, 2), [xp], step_scale, noise_scale, wt, wo, noise, start)
    both = tot + other
    parts = [other] + [shifted(both, "tm", 2 * i) for i in (1, 2, 3)]
    outer, keep, give = conv((0, 3), [xp, up, down], step_scale, noise_scale, wt, wo, noise, start, part, odd)
    msg, give = message(step_scale, guide_scale, odd, cum, parts, mm, give)
    given = other_core(give)
    chip, msg = add_then(keep, given, msg)
    near = shifted(chip, "tm", 2)
    got = lax.all_to_all(msg.reshape(32, MSG, 128), "space", 0, 0, tiled=True)
    two, got = add_then(chip, near, got)
    far = shifted(two, "tm", 4)
    back = project(base, off, cosv, sinv, got.reshape(32 * MSG, 128))
    send, mine, back = send_then(odd, near, far, keep, given, back)
    (send,) = in_hbm(send)
    theirs = other_core(send)
    back = lax.all_to_all(back.reshape(32, 16, 128), "space", 0, 0, tiled=True)
    return final(decoder, odd, back.reshape(512, 128), inner, outer, mine, theirs)


def solution(mesh):
    return jax.shard_map(
        on_device,
        mesh=mesh,
        in_specs=(
            P("tm", None, "space", None, None),
            P("tm", None, "space", None, None),
            P(None, "space", None, None),
            P(),
            P(),
            P("tm", None),
            P(),
            P(),
            P(),
            P("space", None, None),
            P("tm"),
            P("tm"),
            P("tm"),
        ),
        out_specs=P("tm", None, "space", None, None),
        check_vma=False,
    )
```

```python
import functools

import jax
import jax.numpy as jnp
from jax import lax
from jax.experimental import pallas as pl
from jax.experimental.pallas import tpu as pltpu
from jax.sharding import PartitionSpec as P

ANGLES = 180
PROJ = 0.125
NV = 32
NS = 96
WIN = 24
PAD = 168
MSG = 24
F32 = jnp.float32
BF16 = jnp.bfloat16
VMEM = pl.BlockSpec(memory_space=pltpu.VMEM)
SMEM = pl.BlockSpec(memory_space=pltpu.SMEM)
ANY = pl.BlockSpec(memory_space=pl.ANY)
HBM = pl.BlockSpec(memory_space=pltpu.HBM)


def params(mib):
    return pltpu.CompilerParams(vmem_limit_bytes=mib << 20)


def in_hbm(*values):
    return [pltpu.with_memory_space_constraint(v, pltpu.HBM) for v in values]


def cost(flops, size, trans=0):
    return pl.CostEstimate(flops=flops, bytes_accessed=size, transcendentals=trans)


def conv_tables(cw, bias, embed, ow, wt, wo, tall):
    tall[...] = jnp.zeros_like(tall)
    for e in range(3):
        for a in range(3):
            for b in range(3):
                at = (e * 3 + a) * 48 + b * 8
                tall[at : at + 8, 0:64] = 0.5 * cw[9 * a + 3 * b + e].astype(F32)
    both = 0.5 * (bias[...].reshape(1, 64) + embed[...])
    hi = both.astype(BF16).astype(F32)
    mid = (both - hi).astype(BF16).astype(F32)
    for i, piece in enumerate((hi, mid, both - hi - mid)):
        tall[512 + 48 + 4 * i : 512 + 52 + 4 * i, 0:64] = piece
    flat = tall[0:512, :].T[:64]
    shift = tall[512:640, :].T[:64]
    shift = jnp.concatenate([jnp.zeros((64, 384), F32), shift], axis=1)
    for o in range(4):
        moved = flat if o == 0 else pltpu.roll(flat, 8 * o, 1)
        wt[o * 64 : o * 64 + 64, :] = (moved + shift)[:, :448].astype(BF16)
    out = ow[...].astype(F32)
    out = jnp.concatenate([out, out], axis=1)
    out = jnp.concatenate([out] * 4, axis=1)
    lane = lax.broadcasted_iota(jnp.int32, (8, 512), 1) // 64
    own = lane == lax.broadcasted_iota(jnp.int32, (8, 512), 0)
    for c in range(0, 8, 2):
        rows = [jnp.where(own, jnp.broadcast_to(out[i : i + 1], (8, 512)), 0.0) for i in (c, c + 1)]
        wo[c * 8 : c * 8 + 16, :] = jnp.concatenate(rows, axis=0).astype(BF16)


def prep_kernel(*refs):
    source = refs[8]
    xp, top, bottom, cum, tot, mm, wt, wo = refs[9:17]
    dec, scale, guide, meas, cw, bias, embed, ow, traj, sems, scr, tall = refs[17:]
    small = list(zip(refs[:8], (dec, scale, guide, meas, cw, bias, embed, ow)))
    small = [pltpu.make_async_copy(a, b, sems.at[4 + i]) for i, (a, b) in enumerate(small)]
    copies = [pltpu.make_async_copy(source.at[:, :, z], traj.at[z], sems.at[z]) for z in range(4)]
    for copy in copies + small:
        copy.start()
    for copy in small:
        copy.wait()
    conv_tables(cw, bias, embed, ow, wt, wo, tall)
    wk = [scale[k] * guide[k] for k in range(4)]
    mm[...] = jnp.zeros_like(mm)
    for s in range(3):
        x = meas[s]
        stack = jnp.concatenate([x] + [pltpu.roll(x, 128 - 32 * i, 1) for i in range(1, 4)], axis=0)
        mm[pl.ds(s, 32, stride=8), :] = stack.T[:32]
    for z in range(4):
        copies[z].wait()
        run = None
        for k in range(4):
            acc = None
            for c in range(8):
                v = traj[z, k, c].astype(F32)
                scr[k % 2, c * 32 : (c + 1) * 32, :] = v
                term = dec[c] * v
                acc = term if acc is None else acc + term
            acc = wk[k] * acc
            run = acc if run is None else run + acc
            cum[k, z * 16 : z * 16 + 16, :] = run[:16]
            cum[k, 64 + z * 16 : 64 + z * 16 + 16, :] = run[16:]
            for y in range(0, 32, 2):
                rows = jnp.concatenate(
                    [scr[k % 2, pl.ds(y, 8, stride=32), :], scr[k % 2, pl.ds(y + 1, 8, stride=32), :]], axis=0
                )
                rows = rows.astype(BF16)
                xp[k, z, y * 8 : y * 8 + 16, :] = rows
                if z == 0:
                    bottom[k, y * 8 : y * 8 + 16, :] = rows
                if z == 3:
                    top[k, y * 8 : y * 8 + 16, :] = rows
        tot[z * 16 : z * 16 + 16, :] = run[:16]
        tot[64 + z * 16 : 64 + z * 16 + 16, :] = run[16:]
    tot[128:136, :] = jnp.full((8, 128), wk[0] + wk[1] + wk[2] + wk[3], F32)


def prep(dec, scale, guide, meas, conv_weight, conv_bias, step_embed, out_weight, traj):
    conv_weight = conv_weight.swapaxes(1, 2)
    return pl.pallas_call(
        prep_kernel,
        out_shape=(
            jax.ShapeDtypeStruct((4, 4, 256, 128), BF16),
            jax.ShapeDtypeStruct((4, 256, 128), BF16),
            jax.ShapeDtypeStruct((4, 256, 128), BF16),
            jax.ShapeDtypeStruct((4, 128, 128), F32),
            jax.ShapeDtypeStruct((136, 128), F32),
            jax.ShapeDtypeStruct((256, 128), F32),
            jax.ShapeDtypeStruct((256, 448), BF16),
            jax.ShapeDtypeStruct((64, 512), BF16),
        ),
        in_specs=[HBM] * 9,
        out_specs=(VMEM,) * 8,
        scratch_shapes=[
            pltpu.SMEM((8,), F32),
            pltpu.SMEM((4,), F32),
            pltpu.SMEM((4,), F32),
            pltpu.VMEM((3, 32, 128), F32),
            pltpu.VMEM((27, 8, 64), BF16),
            pltpu.VMEM((64,), F32),
            pltpu.VMEM((4, 64), F32),
            pltpu.VMEM((8, 64), BF16),
            pltpu.VMEM((4, 4, 8, 32, 128), BF16),
            pltpu.SemaphoreType.DMA((12,)),
            pltpu.VMEM((2, 256, 128), F32),
            pltpu.VMEM((640, 128), F32),
        ],
        compiler_params=params(16),
        cost_estimate=cost(4_000_000, 2_600_000),
        name="prep",
    )(*in_hbm(dec, scale, guide, meas, conv_weight, conv_bias, step_embed, out_weight, traj))


def message_kernel(scale, guide, odd, cum, other, one, two, three, mm, after, msg):
    wk = [scale[k] * guide[k] for k in range(4)]
    before = jnp.where(odd[0] == 0, 0.0, other[...]) + (one[...] + two[...] + three[...])
    for k in range(4):
        flipped = (cum[k] + before[:128]).T
        for i in range(4):
            msg[pl.ds(4 * i + k, 32, stride=MSG), :] = flipped[32 * i : 32 * i + 32]
    sub = lax.broadcasted_iota(jnp.int32, (8, 128), 0)
    w = before[128:136]
    for k in range(4):
        w = w + jnp.where(sub % 4 >= k, wk[k], 0.0)
    for d in range(32):
        msg[d * MSG + 16 : d * MSG + 24, :] = jnp.where(sub >= 4, w, mm[d * 8 : d * 8 + 8, :])


def message(scale, guide, odd, cum, parts, mm, after):
    return pl.pallas_call(
        message_kernel,
        out_shape=jax.ShapeDtypeStruct((32 * MSG, 128), F32),
        in_specs=[SMEM, SMEM, SMEM] + [VMEM] * 6 + [ANY],
        out_specs=VMEM,
        compiler_params=params(8),
        cost_estimate=cost(100_000, 900_000),
        name="message",
    )(*in_hbm(scale, guide), odd, cum, *parts, mm, after)


def conv_kernel(zs, refs_of, ns_in, scale, nscale, *refs):
    ins, rest = list(refs[:ns_in]), refs[ns_in:]
    wt, wo, noise_from, start_from = rest[:4]
    extra = rest[4:]
    done = None
    fetched = {}
    if ns_in == 3:
        done_from, odd, extra = extra[:2], extra[2], extra[4:]
        run_ref, tot_ref, give_ref, scr, noise, start, sems, held_planes, done, begun, more_sems = extra
        sources = [ins[1], ins[0].at[:, 0], ins[0].at[:, 1], ins[0].at[:, 2], ins[0].at[:, 3], ins[2]]
        for p, source in enumerate(sources):
            fetched[p] = pltpu.make_async_copy(source, held_planes.at[p], more_sems.at[p])
            fetched[p].start()
        for i in range(2):
            fetched[6 + i] = pltpu.make_async_copy(done_from[i].at[3, :, 0], done.at[i], more_sems.at[6 + i])
            fetched[8 + i] = pltpu.make_async_copy(start_from.at[:, 1 + i], begun.at[i], more_sems.at[8 + i])
            fetched[6 + i].start()
            fetched[8 + i].start()
        ins = [held_planes]
    else:
        run_ref, scr, noise, start, sems = extra[1:] if len(extra) == 6 else extra

    def put(value, z, rows):
        if done is not None:
            low, high = value[:4], value[4:]
            tot_ref[:, z, rows, :] = jnp.where(odd[0] == 0, low, high)
            give_ref[:, z, rows, :] = jnp.where(odd[0] == 0, high, low)

    copies = []
    for i, z in enumerate(zs):
        copies.append(pltpu.make_async_copy(noise_from.at[:, :, z], noise.at[i], sems.at[0, i]))
        copies.append(pltpu.make_async_copy(start_from.at[:, z], start.at[i], sems.at[1, i]))
    for copy in copies:
        copy.start()
    planes = refs_of(ins)
    lane = lax.broadcasted_iota(jnp.int32, (16, 128), 1)
    zero = jnp.zeros((8, 128), BF16)
    for p, plane in enumerate(planes):
        if fetched:
            fetched[p].wait()
        for k in range(4):
            for e in range(3):
                scr[p, e, k, 0:16, :] = jnp.zeros((16, 128), BF16)
                scr[p, e, k, 256:272, :] = jnp.zeros((16, 128), BF16)
            held = zero.astype(F32)
            rows = plane(k)
            for r in range(17):
                if r < 16:
                    cur = rows(r).astype(F32)
                    v = jnp.concatenate([held, cur[:8]], axis=0)
                    held = cur[8:]
                else:
                    v = jnp.concatenate([held, zero.astype(F32)], axis=0)
                left = jnp.where(lane == 0, 0.0, pltpu.roll(v, 1, 1))
                right = jnp.where(lane == 127, 0.0, pltpu.roll(v, 127, 1))
                scr[p, 0, k, r * 16 : r * 16 + 16, :] = left.astype(BF16)
                scr[p, 1, k, r * 16 : r * 16 + 16, :] = v.astype(BF16)
                scr[p, 2, k, r * 16 : r * 16 + 16, :] = right.astype(BF16)
    row = lax.broadcasted_iota(jnp.int32, (16, 512), 0)
    kk = lax.broadcasted_iota(jnp.int32, (16, 512), 1) // 128
    ones = jnp.where((row < 12) & (row % 4 == kk), 1.0, 0.0).astype(BF16)

    for copy in copies:
        copy.wait()

    def block(step, carry):
        zi, yb = step // 2, step % 2
        first = 3 * zi
        zrow = pl.multiple_of(yb * 16, 16)
        grain = [noise[zi, k, :, pl.ds(zrow, 16), :].astype(F32) for k in range(4)]
        begin = start[zi, :, pl.ds(zrow, 16), :]
        for half in range(2):
            hidden = []
            for jj in range(2):
                top = pl.multiple_of((yb * 4 + half * 2 + jj) * 32, 32)
                parts = []
                for e in range(3):
                    for a in range(3):
                        parts.append(
                            jnp.concatenate([scr[first + a, e, k, pl.ds(top, 48), :] for k in range(4)], axis=1)
                        )
                parts.append(ones)
                patch = jnp.concatenate(parts, axis=0)
                pre = jnp.dot(wt[...], patch, preferred_element_type=F32)
                hidden.append((pre + pre * jnp.tanh(pre)).astype(BF16))
            eps = jnp.dot(wo[...], jnp.concatenate(hidden, axis=0), preferred_element_type=F32)
            at = pl.multiple_of(yb * 16 + half * 8, 8)
            acc = None
            for k in range(4):
                term = scale[k] * eps[:, k * 128 : k * 128 + 128].reshape(8, 8, 128)
                term = term + nscale[k] * grain[k][:, half * 8 : half * 8 + 8]
                acc = term if acc is None else acc + term
                run_ref[k, :, zi, pl.ds(at, 8), :] = acc + begin[:, half * 8 : half * 8 + 8]
            put(acc, 3 * zi, pl.ds(at, 8))
        return carry

    lax.fori_loop(0, 2 * len(zs), block, 0)
    if done is not None:
        for z in range(2):
            fetched[6 + z].wait()
            fetched[8 + z].wait()
            put(done[z] - begun[z], 1 + z, pl.ds(0, 32))


def conv(zs, planes, scale, nscale, wt, wo, noise, start, done=None, odd=None, after=None):
    inner = len(zs) == 1

    def refs_of(ins):
        own = ins[0]

        def of(z):
            if inner:
                return lambda k: (lambda r: own[k, zs[0] - 1 + z, r * 16 : r * 16 + 16, :])
            return lambda k: (lambda r: own[z, k, r * 16 : r * 16 + 16, :])

        return [of(z) for z in range(3 * len(zs))]

    more = [] if after is None else [after]
    more = more if done is None else [*done, odd, after]
    extra = []
    if not inner:
        planes = in_hbm(*planes)
        extra = [
            pltpu.VMEM((6, 4, 256, 128), BF16),
            pltpu.VMEM((2, 8, 32, 128), F32),
            pltpu.VMEM((2, 8, 32, 128), F32),
            pltpu.SemaphoreType.DMA((10,)),
        ]
    sums = []
    if done is not None:
        sums = [jax.ShapeDtypeStruct((4, 4, 32, 128), F32)] * 2
    return pl.pallas_call(
        functools.partial(conv_kernel, zs, refs_of, len(planes)),
        out_shape=(
            jax.ShapeDtypeStruct((4, 8, len(zs), 32, 128), F32),
            *sums,
        ),
        in_specs=[SMEM, SMEM]
        + [VMEM if inner else HBM] * len(planes)
        + [VMEM, VMEM, HBM, HBM]
        + ([ANY, ANY, SMEM, ANY] if done is not None else [ANY] * len(more)),
        out_specs=(VMEM,) * (1 + len(sums)),
        scratch_shapes=[
            pltpu.VMEM((3 * len(zs), 3, 4, 272, 128), BF16),
            pltpu.VMEM((len(zs), 4, 8, 32, 128), BF16),
            pltpu.VMEM((len(zs), 8, 32, 128), F32),
            pltpu.SemaphoreType.DMA((2, 2)),
            *extra,
        ],
        compiler_params=params(16),
        cost_estimate=cost(3_000_000_000 * len(zs), 2_000_000 * len(zs), 1_000_000 * len(zs)),
        name=f"conv_{zs[0]}" if inner else "conv_outer",
    )(*in_hbm(scale, nscale), *planes, wt, wo, *in_hbm(noise, start), *more)


def project_kernel(base, off, cosv, sinv, got, out, table, sino, meas, seen_hi, seen_lo):
    lane = lax.broadcasted_iota(jnp.int32, (16, 128), 1)
    low = lane < 64
    sino[...] = jnp.zeros_like(sino)
    for d in range(32):
        meas[3 * d : 3 * d + 3, :] = got[d * MSG + 16 : d * MSG + 19, :]
    cell = lax.broadcasted_iota(jnp.int32, (8, 256), 1)
    dy = (cell % 16).astype(F32)
    dz = (cell // 16).astype(F32)
    sub = lax.broadcasted_iota(jnp.int32, (8, 256), 0).astype(F32)

    def where_rows(t, v):
        return v * PAD + 24 + base[t * NV + v]

    def forward(zt, carry):
        slab = [got[pl.ds(pl.multiple_of((4 * zt + i) * MSG, 8), 16), :] for i in range(4)]
        flip = [pltpu.roll(s, 64, 1) for s in slab]
        tiles = [
            jnp.concatenate([jnp.where(low, slab[0], flip[1]), jnp.where(low, slab[2], flip[3])], axis=1),
            jnp.concatenate([jnp.where(low, flip[0], slab[1]), jnp.where(low, flip[2], slab[3])], axis=1),
        ]
        for yt in range(2):
            t = zt * 2 + yt
            image = tiles[yt]
            hi = image.astype(BF16)
            lo = (image - hi.astype(F32)).astype(BF16)
            gap = jnp.zeros((16, 256), BF16)
            columns = jnp.concatenate([gap, gap, hi, gap, lo, gap, gap, gap], axis=0)
            columns = jnp.concatenate([columns, columns], axis=1)
            for v in range(0, NV, 2):
                rows = []
                for u in (v, v + 1):
                    at = dy * cosv[u] + dz * sinv[u] + off[t * NV + u]
                    for b in range(3):
                        rows.append(jnp.maximum(0.0, 1.0 - jnp.abs(at - (sub + 8.0 * b))))
                hat = jnp.concatenate(rows, axis=0)
                top = hat.astype(BF16)
                rest = (hat - top.astype(F32)).astype(BF16)
                table[t, v * WIN : (v + 2) * WIN, 0:256] = top
                table[t, v * WIN : (v + 2) * WIN, 256:512] = rest
            sums = lax.dot_general(table[t], columns, (((1,), (1,)), ((), ())), preferred_element_type=F32)
            for v in range(NV):
                at = pl.ds(where_rows(t, v), WIN)
                sino[at, :] = sino[at, :] + sums[v * WIN : (v + 1) * WIN]
        return carry

    lax.fori_loop(0, 8, forward, 0)

    whole = meas[...]
    whole_hi = whole.astype(BF16).astype(F32)
    seen_hi[...] = whole_hi
    seen_lo[...] = pltpu.roll(whole - whole_hi, 1, 1)
    wide = lax.broadcasted_iota(jnp.int32, (8, 128), 1)
    is_hi = (wide >= 32) & (wide < 48)
    is_lo = (wide >= 64) & (wide < 80)
    is_seen = wide % 32 == 24
    is_rest = wide % 32 == 25

    def misfit(v):
        at = pl.multiple_of(v * PAD, 8)
        turn = lax.rem(128 + 24 - v, 128)
        for r in range(0, NS, 8):
            rows = sino[pl.ds(at + 24 + r, 8), :]
            rows = PROJ * (rows + pltpu.roll(rows, 96, 1))
            hi = rows.astype(BF16).astype(F32)
            lo = pltpu.roll(rows - hi, 32, 1)
            top = pltpu.roll(seen_hi[r : r + 8, :], turn, 1)
            rest = pltpu.roll(seen_lo[r : r + 8, :], turn, 1)
            spread = jnp.where(is_hi, hi, jnp.where(is_lo, lo, 0.0))
            sino[pl.ds(at + 24 + r, 8), :] = jnp.where(is_seen, top, jnp.where(is_rest, rest, spread))
        sino[pl.ds(at, 24), :] = jnp.zeros((24, 128), F32)
        sino[pl.ds(at + 120, 48), :] = jnp.zeros((48, 128), F32)

    def misfits(group, carry):
        for v in range(16):
            misfit(group * 16 + v)
        return carry

    lax.fori_loop(0, NV // 16, misfits, 0)

    upper = lax.broadcasted_iota(jnp.int32, (8, 256), 0) < 4
    wk = got[16:24, :]
    wk = jnp.where(upper[:, :128], pltpu.roll(wk, 4, 0), wk)
    wk = jnp.concatenate([wk, wk], axis=1)

    def backward(zt, carry):
        tiles = []
        for yt in range(2):
            t = zt * 2 + yt
            rows = jnp.concatenate([sino[pl.ds(where_rows(t, v), WIN), :] for v in range(NV)], axis=0)
            sums = lax.dot_general(
                rows.astype(BF16), table[t], (((0,), (0,)), ((), ())), preferred_element_type=F32
            )
            sums = sums[:, :256] + sums[:, 256:]
            pair = []
            for h in range(2):
                seen = [
                    sums[24 + 32 * i : 25 + 32 * i] + sums[25 + 32 * i : 26 + 32 * i] for i in (2 * h, 2 * h + 1)
                ]
                ours = sums[32 + 8 * h : 40 + 8 * h] + sums[64 + 8 * h : 72 + 8 * h]
                pair.append(PROJ * (ours - wk * jnp.where(upper, seen[0], seen[1])))
            tiles.append(jnp.concatenate(pair, axis=0))
        for h in range(2):
            a, b = (tile[:, 128 * h : 128 * h + 128] for tile in tiles)
            at = pl.multiple_of((4 * zt + 2 * h) * 16, 16)
            out[pl.ds(at, 16), :] = jnp.where(low, a, pltpu.roll(b, 64, 1))
            out[pl.ds(at + 16, 16), :] = jnp.where(low, pltpu.roll(a, 64, 1), b)
        return carry

    lax.fori_loop(0, 8, backward, 0)


def project(base, off, cosv, sinv, got):
    return pl.pallas_call(
        project_kernel,
        out_shape=jax.ShapeDtypeStruct((512, 128), F32),
        in_specs=[SMEM, SMEM, SMEM, SMEM, VMEM],
        out_specs=VMEM,
        scratch_shapes=[
            pltpu.VMEM((16, NV * WIN, 512), BF16),
            pltpu.VMEM((NV * PAD, 128), F32),
            pltpu.VMEM((NS, 128), F32),
            pltpu.VMEM((NS, 128), F32),
            pltpu.VMEM((NS, 128), F32),
        ],
        compiler_params=params(22),
        cost_estimate=cost(8_000_000_000, 2_000_000),
        name="project",
    )(base, off, cosv, sinv, got)


def final_kernel(dec, odd, back, one, two, outer, mine, theirs, new):
    k = pl.program_id(0)
    columns = jnp.concatenate([back[pl.ds(4 * i + k, 32, stride=16), :] for i in range(4)], axis=0)
    cells = columns.T
    for z in range(4):
        guide = jnp.concatenate([cells[z * 16 : z * 16 + 16], cells[64 + z * 16 : 80 + z * 16]], axis=0)
        for c in range(8):
            own = (one, two)[z - 1][0, c, 0] if z in (1, 2) else outer[0, c, z // 3]
            before = jnp.where(odd[0] == c // 4, mine[c % 4, z], theirs[c % 4, z])
            new[0, c, z] = own + before - dec[c] * guide


def final(dec, odd, back, one, two, outer, mine, theirs):
    whole = pl.BlockSpec((512, 128), lambda k: (0, 0))
    part = pl.BlockSpec((1, 8, 2, 32, 128), lambda k: (k, 0, 0, 0, 0))
    single = pl.BlockSpec((1, 8, 1, 32, 128), lambda k: (k, 0, 0, 0, 0))
    half = pl.BlockSpec((4, 4, 32, 128), lambda k: (0, 0, 0, 0))
    return pl.pallas_call(
        final_kernel,
        grid=(4,),
        out_shape=jax.ShapeDtypeStruct((4, 8, 4, 32, 128), F32),
        in_specs=[SMEM, SMEM, whole, single, single, part, half, half],
        out_specs=pl.BlockSpec((1, 8, 4, 32, 128), lambda k: (k, 0, 0, 0, 0)),
        compiler_params=params(16),
        cost_estimate=cost(2_000_000, 5_000_000),
        name="final",
    )(*in_hbm(dec), odd, back, one, two, outer, *in_hbm(mine), theirs)


def add_kernel(a, b, held, out, passed):
    out[...] = a[...] + b[...]


def add_then(a, b, held):
    return pl.pallas_call(
        add_kernel,
        out_shape=(jax.ShapeDtypeStruct(a.shape, F32), jax.ShapeDtypeStruct(held.shape, held.dtype)),
        in_specs=[VMEM, VMEM, ANY],
        out_specs=(VMEM, ANY),
        input_output_aliases={2: 1},
        compiler_params=params(4),
        cost_estimate=cost(100_000, 800_000),
        name="add_then",
    )(a, b, held)


def send_kernel(odd, near, far, keep, given, send, mine):
    first = odd[0] == 0
    chips = near[...] + far[...]
    send[...] = chips + jnp.where(first, keep[...], 0.0)
    mine[...] = chips + jnp.where(first, 0.0, given[...])


def send_on(odd, near, far, keep, given):
    return pl.pallas_call(
        send_kernel,
        out_shape=(jax.ShapeDtypeStruct(near.shape, F32),) * 2,
        in_specs=[SMEM, VMEM, VMEM, VMEM, VMEM],
        out_specs=(VMEM, VMEM),
        compiler_params=params(4),
        cost_estimate=cost(100_000, 1_500_000),
        name="send_on",
    )(odd, near, far, keep, given)


def shifted(value, axis, step):
    count = lax.axis_size(axis)
    return lax.ppermute(value, axis, [(i, i + step) for i in range(count) if 0 <= i + step < count])


def other_core(value):
    return lax.ppermute(value, "tm", [(i, i ^ 1) for i in range(lax.axis_size("tm"))])


def windows(angle_index):
    theta = jnp.pi * angle_index.astype(F32) / ANGLES
    cosv, sinv = jnp.cos(theta), jnp.sin(theta)
    tile = jnp.arange(16)
    z0 = (16 * (tile // 2)).astype(F32) - 63.5
    y0 = (16 * (tile % 2)).astype(F32) - 15.5
    corner = y0[:, None] * cosv[None] + z0[:, None] * sinv[None] + 47.5
    least = corner + jnp.minimum(0.0, 15.0 * cosv)[None] + jnp.minimum(0.0, 15.0 * sinv)[None]
    base = jnp.floor(least - 0.001)
    return base.astype(jnp.int32).reshape(512), (corner - base).reshape(512), cosv, sinv


def on_device(
    trajectory,
    noise,
    start,
    conv_weight,
    conv_bias,
    step_embed,
    out_weight,
    decoder,
    angle_index,
    measured,
    step_scale,
    guide_scale,
    noise_scale,
):
    odd = (lax.axis_index("tm") % 2).reshape(1)
    xp, top, bottom, cum, tot, mm, wt, wo = prep(
        decoder, step_scale, guide_scale, measured, conv_weight, conv_bias, step_embed, out_weight, trajectory
    )
    up = shifted(top, "space", 1)
    down = shifted(bottom, "space", -1)
    other = other_core(tot)
    base, off, cosv, sinv = windows(angle_index)
    own = (step_scale, noise_scale, wt, wo, noise, start)
    (one,) = conv((1,), [xp], *own)
    both = tot + other
    parts = [other] + [shifted(both, "tm", 2 * i) for i in (1, 2, 3)]
    (two,) = conv((2,), [xp], *own, after=both)
    msg = message(step_scale, guide_scale, odd, cum, parts, mm, two)
    got = lax.all_to_all(msg.reshape(32, MSG, 128), "space", 0, 0, tiled=True)
    outer, keep, give = conv((0, 3), [xp, up, down], *own, (one, two), odd, msg)
    given = other_core(give)
    chip, got = add_then(keep, given, got)
    near = shifted(chip, "tm", 2)
    back = project(base, off, cosv, sinv, got.reshape(32 * MSG, 128))
    chips, back = add_then(chip, near, back)
    far = shifted(chips, "tm", 4)
    send, mine = send_on(odd, near, far, keep, given)
    theirs = other_core(send)
    back = lax.all_to_all(back.reshape(32, 16, 128), "space", 0, 0, tiled=True)
    return final(decoder, odd, back.reshape(512, 128), one, two, outer, mine, theirs)


def solution(mesh):
    return jax.shard_map(
        on_device,
        mesh=mesh,
        in_specs=(
            P("tm", None, "space", None, None),
            P("tm", None, "space", None, None),
            P(None, "space", None, None),
            P(),
            P(),
            P("tm", None),
            P(),
            P(),
            P(),
            P("space", None, None),
            P("tm"),
            P("tm"),
            P("tm"),
        ),
        out_specs=P("tm", None, "space", None, None),
        check_vma=False,
    )
```

```python
import functools

import jax
import jax.numpy as jnp
from jax import lax
from jax.experimental import pallas as pl
from jax.experimental.pallas import tpu as pltpu
from jax.sharding import PartitionSpec as P

ANGLES = 180
PROJ = 0.125
NV = 32
NS = 96
WIN = 24
PAD = 168
MSG = 24
F32 = jnp.float32
BF16 = jnp.bfloat16
VMEM = pl.BlockSpec(memory_space=pltpu.VMEM)
SMEM = pl.BlockSpec(memory_space=pltpu.SMEM)
ANY = pl.BlockSpec(memory_space=pl.ANY)
HBM = pl.BlockSpec(memory_space=pltpu.HBM)


def params(mib):
    return pltpu.CompilerParams(vmem_limit_bytes=mib << 20)


def in_hbm(*values):
    return [pltpu.with_memory_space_constraint(v, pltpu.HBM) for v in values]


def cost(flops, size, trans=0):
    return pl.CostEstimate(flops=flops, bytes_accessed=size, transcendentals=trans)


def conv_tables(cw, bias, embed, ow, wt, wo, tall):
    tall[...] = jnp.zeros_like(tall)
    for e in range(3):
        for a in range(3):
            for b in range(3):
                at = (e * 3 + a) * 48 + b * 8
                tall[at : at + 8, 0:64] = 0.5 * cw[9 * a + 3 * b + e].astype(F32)
    both = 0.5 * (bias[...].reshape(1, 64) + embed[...])
    hi = both.astype(BF16).astype(F32)
    mid = (both - hi).astype(BF16).astype(F32)
    for i, piece in enumerate((hi, mid, both - hi - mid)):
        tall[512 + 48 + 4 * i : 512 + 52 + 4 * i, 0:64] = piece
    flat = tall[0:512, :].T[:64]
    shift = tall[512:640, :].T[:64]
    shift = jnp.concatenate([jnp.zeros((64, 384), F32), shift], axis=1)
    for o in range(4):
        moved = flat if o == 0 else pltpu.roll(flat, 8 * o, 1)
        wt[o * 64 : o * 64 + 64, :] = (moved + shift)[:, :448].astype(BF16)
    out = ow[...].astype(F32)
    out = jnp.concatenate([out, out], axis=1)
    out = jnp.concatenate([out] * 4, axis=1)
    lane = lax.broadcasted_iota(jnp.int32, (8, 512), 1) // 64
    own = lane == lax.broadcasted_iota(jnp.int32, (8, 512), 0)
    for c in range(0, 8, 2):
        rows = [jnp.where(own, jnp.broadcast_to(out[i : i + 1], (8, 512)), 0.0) for i in (c, c + 1)]
        wo[c * 8 : c * 8 + 16, :] = jnp.concatenate(rows, axis=0).astype(BF16)


def prep_kernel(*refs):
    source = refs[8]
    xp, top, bottom, cum, tot, mm, wt, wo = refs[9:17]
    dec, scale, guide, meas, cw, bias, embed, ow, traj, sems, scr, tall = refs[17:]
    small = list(zip(refs[:8], (dec, scale, guide, meas, cw, bias, embed, ow)))
    small = [pltpu.make_async_copy(a, b, sems.at[4 + i]) for i, (a, b) in enumerate(small)]
    copies = [pltpu.make_async_copy(source.at[:, :, z], traj.at[z], sems.at[z]) for z in range(4)]
    for copy in copies + small:
        copy.start()
    for copy in small:
        copy.wait()
    conv_tables(cw, bias, embed, ow, wt, wo, tall)
    wk = [scale[k] * guide[k] for k in range(4)]
    mm[...] = jnp.zeros_like(mm)
    for s in range(3):
        x = meas[s]
        stack = jnp.concatenate([x] + [pltpu.roll(x, 128 - 32 * i, 1) for i in range(1, 4)], axis=0)
        mm[pl.ds(s, 32, stride=8), :] = stack.T[:32]
    for z in range(4):
        copies[z].wait()
        run = None
        for k in range(4):
            acc = None
            for c in range(8):
                v = traj[z, k, c].astype(F32)
                scr[k % 2, c * 32 : (c + 1) * 32, :] = v
                term = dec[c] * v
                acc = term if acc is None else acc + term
            acc = wk[k] * acc
            run = acc if run is None else run + acc
            cum[k, z * 16 : z * 16 + 16, :] = run[:16]
            cum[k, 64 + z * 16 : 64 + z * 16 + 16, :] = run[16:]
            for y in range(0, 32, 2):
                rows = jnp.concatenate(
                    [scr[k % 2, pl.ds(y, 8, stride=32), :], scr[k % 2, pl.ds(y + 1, 8, stride=32), :]], axis=0
                )
                rows = rows.astype(BF16)
                xp[k, z, y * 8 : y * 8 + 16, :] = rows
                if z == 0:
                    bottom[k, y * 8 : y * 8 + 16, :] = rows
                if z == 3:
                    top[k, y * 8 : y * 8 + 16, :] = rows
        tot[z * 16 : z * 16 + 16, :] = run[:16]
        tot[64 + z * 16 : 64 + z * 16 + 16, :] = run[16:]
    tot[128:136, :] = jnp.full((8, 128), wk[0] + wk[1] + wk[2] + wk[3], F32)


def prep(dec, scale, guide, meas, conv_weight, conv_bias, step_embed, out_weight, traj):
    conv_weight = conv_weight.swapaxes(1, 2)
    return pl.pallas_call(
        prep_kernel,
        out_shape=(
            jax.ShapeDtypeStruct((4, 4, 256, 128), BF16),
            jax.ShapeDtypeStruct((4, 256, 128), BF16),
            jax.ShapeDtypeStruct((4, 256, 128), BF16),
            jax.ShapeDtypeStruct((4, 128, 128), F32),
            jax.ShapeDtypeStruct((136, 128), F32),
            jax.ShapeDtypeStruct((256, 128), F32),
            jax.ShapeDtypeStruct((256, 448), BF16),
            jax.ShapeDtypeStruct((64, 512), BF16),
        ),
        in_specs=[HBM] * 9,
        out_specs=(VMEM,) * 8,
        scratch_shapes=[
            pltpu.SMEM((8,), F32),
            pltpu.SMEM((4,), F32),
            pltpu.SMEM((4,), F32),
            pltpu.VMEM((3, 32, 128), F32),
            pltpu.VMEM((27, 8, 64), BF16),
            pltpu.VMEM((64,), F32),
            pltpu.VMEM((4, 64), F32),
            pltpu.VMEM((8, 64), BF16),
            pltpu.VMEM((4, 4, 8, 32, 128), BF16),
            pltpu.SemaphoreType.DMA((12,)),
            pltpu.VMEM((2, 256, 128), F32),
            pltpu.VMEM((640, 128), F32),
        ],
        compiler_params=params(16),
        cost_estimate=cost(4_000_000, 2_600_000),
        name="prep",
    )(*in_hbm(dec, scale, guide, meas, conv_weight, conv_bias, step_embed, out_weight, traj))


def message_kernel(scale, guide, odd, cum, other, one, two, three, mm, after, msg):
    wk = [scale[k] * guide[k] for k in range(4)]
    before = jnp.where(odd[0] == 0, 0.0, other[...]) + (one[...] + two[...] + three[...])
    for k in range(4):
        flipped = (cum[k] + before[:128]).T
        for i in range(4):
            msg[pl.ds(4 * i + k, 32, stride=MSG), :] = flipped[32 * i : 32 * i + 32]
    sub = lax.broadcasted_iota(jnp.int32, (8, 128), 0)
    w = before[128:136]
    for k in range(4):
        w = w + jnp.where(sub % 4 >= k, wk[k], 0.0)
    for d in range(32):
        msg[d * MSG + 16 : d * MSG + 24, :] = jnp.where(sub >= 4, w, mm[d * 8 : d * 8 + 8, :])


def message(scale, guide, odd, cum, parts, mm, after):
    return pl.pallas_call(
        message_kernel,
        out_shape=jax.ShapeDtypeStruct((32 * MSG, 128), F32),
        in_specs=[SMEM, SMEM, SMEM] + [VMEM] * 6 + [ANY],
        out_specs=VMEM,
        compiler_params=params(8),
        cost_estimate=cost(100_000, 900_000),
        name="message",
    )(*in_hbm(scale, guide), odd, cum, *parts, mm, after)


def conv_kernel(zs, refs_of, ns_in, scale, nscale, *refs):
    ins, rest = list(refs[:ns_in]), refs[ns_in:]
    wt, wo, noise_from, start_from = rest[:4]
    extra = rest[4:]
    done = None
    fetched = {}
    if ns_in == 3:
        done_from, odd, extra = extra[:2], extra[2], extra[4:]
        run_ref, tot_ref, give_ref, scr, noise, start, sems, held_planes, done, begun, more_sems = extra
        sources = [ins[1], ins[0].at[:, 0], ins[0].at[:, 1], ins[0].at[:, 2], ins[0].at[:, 3], ins[2]]
        for p, source in enumerate(sources):
            fetched[p] = pltpu.make_async_copy(source, held_planes.at[p], more_sems.at[p])
            fetched[p].start()
        for i in range(2):
            fetched[6 + i] = pltpu.make_async_copy(done_from[i].at[3, :, 0], done.at[i], more_sems.at[6 + i])
            fetched[8 + i] = pltpu.make_async_copy(start_from.at[:, 1 + i], begun.at[i], more_sems.at[8 + i])
            fetched[6 + i].start()
            fetched[8 + i].start()
        ins = [held_planes]
    else:
        run_ref, scr, noise, start, sems = extra[1:] if len(extra) == 6 else extra

    def put(value, z, rows):
        if done is not None:
            low, high = value[:4], value[4:]
            tot_ref[:, z, rows, :] = jnp.where(odd[0] == 0, low, high)
            give_ref[:, z, rows, :] = jnp.where(odd[0] == 0, high, low)

    copies = []
    for i, z in enumerate(zs):
        copies.append(pltpu.make_async_copy(noise_from.at[:, :, z], noise.at[i], sems.at[0, i]))
        copies.append(pltpu.make_async_copy(start_from.at[:, z], start.at[i], sems.at[1, i]))
    for copy in copies:
        copy.start()
    planes = refs_of(ins)
    lane = lax.broadcasted_iota(jnp.int32, (16, 128), 1)
    zero = jnp.zeros((8, 128), BF16)
    for p, plane in enumerate(planes):
        if fetched:
            fetched[p].wait()
        for k in range(4):
            for e in range(3):
                scr[p, e, k, 0:16, :] = jnp.zeros((16, 128), BF16)
                scr[p, e, k, 256:272, :] = jnp.zeros((16, 128), BF16)
            held = zero.astype(F32)
            rows = plane(k)
            for r in range(17):
                if r < 16:
                    cur = rows(r).astype(F32)
                    v = jnp.concatenate([held, cur[:8]], axis=0)
                    held = cur[8:]
                else:
                    v = jnp.concatenate([held, zero.astype(F32)], axis=0)
                left = jnp.where(lane == 0, 0.0, pltpu.roll(v, 1, 1))
                right = jnp.where(lane == 127, 0.0, pltpu.roll(v, 127, 1))
                scr[p, 0, k, r * 16 : r * 16 + 16, :] = left.astype(BF16)
                scr[p, 1, k, r * 16 : r * 16 + 16, :] = v.astype(BF16)
                scr[p, 2, k, r * 16 : r * 16 + 16, :] = right.astype(BF16)
    row = lax.broadcasted_iota(jnp.int32, (16, 512), 0)
    kk = lax.broadcasted_iota(jnp.int32, (16, 512), 1) // 128
    ones = jnp.where((row < 12) & (row % 4 == kk), 1.0, 0.0).astype(BF16)

    lazy = len(zs) == 1
    if not lazy:
        for copy in copies:
            copy.wait()

    def block(step, carry):
        zi, yb = step // 2, step % 2
        first = 3 * zi
        zrow = pl.multiple_of(yb * 16, 16)
        for half in range(2):
            hidden = []
            for jj in range(2):
                top = pl.multiple_of((yb * 4 + half * 2 + jj) * 32, 32)
                parts = []
                for e in range(3):
                    for a in range(3):
                        parts.append(
                            jnp.concatenate([scr[first + a, e, k, pl.ds(top, 48), :] for k in range(4)], axis=1)
                        )
                parts.append(ones)
                patch = jnp.concatenate(parts, axis=0)
                pre = jnp.dot(wt[...], patch, preferred_element_type=F32)
                hidden.append((pre + pre * jnp.tanh(pre)).astype(BF16))
            eps = jnp.dot(wo[...], jnp.concatenate(hidden, axis=0), preferred_element_type=F32)
            at = pl.multiple_of(yb * 16 + half * 8, 8)
            if half == 0:
                if lazy:

                    @pl.when(step == 0)
                    def _():
                        for copy in copies:
                            copy.wait()

                grain = [noise[zi, k, :, pl.ds(zrow, 16), :].astype(F32) for k in range(4)]
                begin = start[zi, :, pl.ds(zrow, 16), :]
            acc = None
            for k in range(4):
                term = scale[k] * eps[:, k * 128 : k * 128 + 128].reshape(8, 8, 128)
                term = term + nscale[k] * grain[k][:, half * 8 : half * 8 + 8]
                acc = term if acc is None else acc + term
                run_ref[k, :, zi, pl.ds(at, 8), :] = acc + begin[:, half * 8 : half * 8 + 8]
            put(acc, 3 * zi, pl.ds(at, 8))
        return carry

    lax.fori_loop(0, 2 * len(zs), block, 0)
    if done is not None:
        for z in range(2):
            fetched[6 + z].wait()
            fetched[8 + z].wait()
            put(done[z] - begun[z], 1 + z, pl.ds(0, 32))


def conv(zs, planes, scale, nscale, wt, wo, noise, start, done=None, odd=None, after=None):
    inner = len(zs) == 1

    def refs_of(ins):
        own = ins[0]

        def of(z):
            if inner:
                return lambda k: (lambda r: own[k, zs[0] - 1 + z, r * 16 : r * 16 + 16, :])
            return lambda k: (lambda r: own[z, k, r * 16 : r * 16 + 16, :])

        return [of(z) for z in range(3 * len(zs))]

    more = [] if after is None else [after]
    more = more if done is None else [*done, odd, after]
    extra = []
    if not inner:
        planes = in_hbm(*planes)
        extra = [
            pltpu.VMEM((6, 4, 256, 128), BF16),
            pltpu.VMEM((2, 8, 32, 128), F32),
            pltpu.VMEM((2, 8, 32, 128), F32),
            pltpu.SemaphoreType.DMA((10,)),
        ]
    sums = []
    if done is not None:
        sums = [jax.ShapeDtypeStruct((4, 4, 32, 128), F32)] * 2
    return pl.pallas_call(
        functools.partial(conv_kernel, zs, refs_of, len(planes)),
        out_shape=(
            jax.ShapeDtypeStruct((4, 8, len(zs), 32, 128), F32),
            *sums,
        ),
        in_specs=[SMEM, SMEM]
        + [VMEM if inner else HBM] * len(planes)
        + [VMEM, VMEM, HBM, HBM]
        + ([ANY, ANY, SMEM, ANY] if done is not None else [ANY] * len(more)),
        out_specs=(VMEM,) * (1 + len(sums)),
        scratch_shapes=[
            pltpu.VMEM((3 * len(zs), 3, 4, 272, 128), BF16),
            pltpu.VMEM((len(zs), 4, 8, 32, 128), BF16),
            pltpu.VMEM((len(zs), 8, 32, 128), F32),
            pltpu.SemaphoreType.DMA((2, 2)),
            *extra,
        ],
        compiler_params=params(16),
        cost_estimate=cost(3_000_000_000 * len(zs), 2_000_000 * len(zs), 1_000_000 * len(zs)),
        name=f"conv_{zs[0]}" if inner else "conv_outer",
    )(*in_hbm(scale, nscale), *planes, wt, wo, *in_hbm(noise, start), *more)


def project_kernel(base, off, cosv, sinv, got, out, table, sino, meas, seen_hi, seen_lo):
    lane = lax.broadcasted_iota(jnp.int32, (16, 128), 1)
    low = lane < 64
    sino[...] = jnp.zeros_like(sino)
    for d in range(32):
        meas[3 * d : 3 * d + 3, :] = got[d * MSG + 16 : d * MSG + 19, :]
    cell = lax.broadcasted_iota(jnp.int32, (8, 256), 1)
    dy = (cell % 16).astype(F32)
    dz = (cell // 16).astype(F32)
    sub = lax.broadcasted_iota(jnp.int32, (8, 256), 0).astype(F32)

    def where_rows(t, v):
        return v * PAD + 24 + base[t * NV + v]

    def forward(zt, carry):
        slab = [got[pl.ds(pl.multiple_of((4 * zt + i) * MSG, 8), 16), :] for i in range(4)]
        flip = [pltpu.roll(s, 64, 1) for s in slab]
        tiles = [
            jnp.concatenate([jnp.where(low, slab[0], flip[1]), jnp.where(low, slab[2], flip[3])], axis=1),
            jnp.concatenate([jnp.where(low, flip[0], slab[1]), jnp.where(low, flip[2], slab[3])], axis=1),
        ]
        for yt in range(2):
            t = zt * 2 + yt
            image = tiles[yt]
            hi = image.astype(BF16)
            lo = (image - hi.astype(F32)).astype(BF16)
            gap = jnp.zeros((16, 256), BF16)
            columns = jnp.concatenate([gap, gap, hi, gap, lo, gap, gap, gap], axis=0)
            columns = jnp.concatenate([columns, columns], axis=1)
            for v in range(0, NV, 2):
                rows = []
                for u in (v, v + 1):
                    at = dy * cosv[u] + dz * sinv[u] + off[t * NV + u]
                    for b in range(3):
                        rows.append(jnp.maximum(0.0, 1.0 - jnp.abs(at - (sub + 8.0 * b))))
                hat = jnp.concatenate(rows, axis=0)
                top = hat.astype(BF16)
                rest = (hat - top.astype(F32)).astype(BF16)
                table[t, v * WIN : (v + 2) * WIN, 0:256] = top
                table[t, v * WIN : (v + 2) * WIN, 256:512] = rest
            sums = lax.dot_general(table[t], columns, (((1,), (1,)), ((), ())), preferred_element_type=F32)
            for v in range(NV):
                at = pl.ds(where_rows(t, v), WIN)
                sino[at, :] = sino[at, :] + sums[v * WIN : (v + 1) * WIN]
        return carry

    lax.fori_loop(0, 8, forward, 0, unroll=2)

    whole = meas[...]
    whole_hi = whole.astype(BF16).astype(F32)
    seen_hi[...] = whole_hi
    seen_lo[...] = pltpu.roll(whole - whole_hi, 1, 1)
    wide = lax.broadcasted_iota(jnp.int32, (8, 128), 1)
    is_hi = (wide >= 32) & (wide < 48)
    is_lo = (wide >= 64) & (wide < 80)
    is_seen = wide % 32 == 24
    is_rest = wide % 32 == 25

    def misfit(v):
        at = pl.multiple_of(v * PAD, 8)
        turn = lax.rem(128 + 24 - v, 128)
        for r in range(0, NS, 8):
            rows = sino[pl.ds(at + 24 + r, 8), :]
            rows = PROJ * (rows + pltpu.roll(rows, 96, 1))
            hi = rows.astype(BF16).astype(F32)
            lo = pltpu.roll(rows - hi, 32, 1)
            top = pltpu.roll(seen_hi[r : r + 8, :], turn, 1)
            rest = pltpu.roll(seen_lo[r : r + 8, :], turn, 1)
            spread = jnp.where(is_hi, hi, jnp.where(is_lo, lo, 0.0))
            sino[pl.ds(at + 24 + r, 8), :] = jnp.where(is_seen, top, jnp.where(is_rest, rest, spread))
        sino[pl.ds(at, 24), :] = jnp.zeros((24, 128), F32)
        sino[pl.ds(at + 120, 48), :] = jnp.zeros((48, 128), F32)

    def misfits(group, carry):
        for v in range(16):
            misfit(group * 16 + v)
        return carry

    lax.fori_loop(0, NV // 16, misfits, 0)

    upper = lax.broadcasted_iota(jnp.int32, (8, 256), 0) < 4
    wk = got[16:24, :]
    wk = jnp.where(upper[:, :128], pltpu.roll(wk, 4, 0), wk)
    wk = jnp.concatenate([wk, wk], axis=1)

    def backward(zt, carry):
        tiles = []
        for yt in range(2):
            t = zt * 2 + yt
            rows = jnp.concatenate([sino[pl.ds(where_rows(t, v), WIN), :] for v in range(NV)], axis=0)
            sums = lax.dot_general(
                rows.astype(BF16), table[t], (((0,), (0,)), ((), ())), preferred_element_type=F32
            )
            sums = sums[:, :256] + sums[:, 256:]
            pair = []
            for h in range(2):
                seen = [
                    sums[24 + 32 * i : 25 + 32 * i] + sums[25 + 32 * i : 26 + 32 * i] for i in (2 * h, 2 * h + 1)
                ]
                ours = sums[32 + 8 * h : 40 + 8 * h] + sums[64 + 8 * h : 72 + 8 * h]
                pair.append(PROJ * (ours - wk * jnp.where(upper, seen[0], seen[1])))
            tiles.append(jnp.concatenate(pair, axis=0))
        for h in range(2):
            a, b = (tile[:, 128 * h : 128 * h + 128] for tile in tiles)
            at = pl.multiple_of((4 * zt + 2 * h) * 16, 16)
            out[pl.ds(at, 16), :] = jnp.where(low, a, pltpu.roll(b, 64, 1))
            out[pl.ds(at + 16, 16), :] = jnp.where(low, pltpu.roll(a, 64, 1), b)
        return carry

    lax.fori_loop(0, 8, backward, 0, unroll=4)


def project(base, off, cosv, sinv, got):
    return pl.pallas_call(
        project_kernel,
        out_shape=jax.ShapeDtypeStruct((512, 128), F32),
        in_specs=[SMEM, SMEM, SMEM, SMEM, VMEM],
        out_specs=VMEM,
        scratch_shapes=[
            pltpu.VMEM((16, NV * WIN, 512), BF16),
            pltpu.VMEM((NV * PAD, 128), F32),
            pltpu.VMEM((NS, 128), F32),
            pltpu.VMEM((NS, 128), F32),
            pltpu.VMEM((NS, 128), F32),
        ],
        compiler_params=params(22),
        cost_estimate=cost(8_000_000_000, 2_000_000),
        name="project",
    )(base, off, cosv, sinv, got)


def final_kernel(dec, odd, back, one, two, outer, mine_from, theirs_from, new, held, mine, theirs, sems):
    parts = [
        pltpu.make_async_copy(mine_from, mine, sems.at[4]),
        pltpu.make_async_copy(theirs_from, theirs, sems.at[5]),
    ]
    for part in parts:
        part.start()
    copies = []
    for k in range(4):
        columns = jnp.concatenate([back[pl.ds(4 * i + k, 32, stride=16), :] for i in range(4)], axis=0)
        cells = columns.T
        if k == 0:
            for part in parts:
                part.wait()
        for z in range(4):
            guide = jnp.concatenate([cells[z * 16 : z * 16 + 16], cells[64 + z * 16 : 80 + z * 16]], axis=0)
            for c in range(8):
                own = (one, two)[z - 1][k, c, 0] if z in (1, 2) else outer[k, c, z // 3]
                before = jnp.where(odd[0] == c // 4, mine[c % 4, z], theirs[c % 4, z])
                held[k, c, z] = own + before - dec[c] * guide
        copies.append(pltpu.make_async_copy(held.at[k], new.at[k], sems.at[k]))
        copies[k].start()
    for copy in copies:
        copy.wait()


def final(dec, odd, back, one, two, outer, mine, theirs):
    return pl.pallas_call(
        final_kernel,
        out_shape=jax.ShapeDtypeStruct((4, 8, 4, 32, 128), F32),
        in_specs=[SMEM, SMEM] + [VMEM] * 4 + [ANY, ANY],
        out_specs=HBM,
        scratch_shapes=[
            pltpu.VMEM((4, 8, 4, 32, 128), F32),
            pltpu.VMEM((4, 4, 32, 128), F32),
            pltpu.VMEM((4, 4, 32, 128), F32),
            pltpu.SemaphoreType.DMA((6,)),
        ],
        compiler_params=params(8),
        cost_estimate=cost(2_000_000, 5_000_000),
        name="final",
    )(*in_hbm(dec), odd, back, one, two, outer, mine, theirs)


def add_kernel(a, b, held, out, passed):
    out[...] = a[...] + b[...]


def add_then(a, b, held):
    return pl.pallas_call(
        add_kernel,
        out_shape=(jax.ShapeDtypeStruct(a.shape, F32), jax.ShapeDtypeStruct(held.shape, held.dtype)),
        in_specs=[VMEM, VMEM, ANY],
        out_specs=(VMEM, ANY),
        input_output_aliases={2: 1},
        compiler_params=params(4),
        cost_estimate=cost(100_000, 800_000),
        name="add_then",
    )(a, b, held)


def send_kernel(odd, near, far, keep, given, send, mine):
    first = odd[0] == 0
    chips = near[...] + far[...]
    send[...] = chips + jnp.where(first, keep[...], 0.0)
    mine[...] = chips + jnp.where(first, 0.0, given[...])


def send_on(odd, near, far, keep, given):
    return pl.pallas_call(
        send_kernel,
        out_shape=(jax.ShapeDtypeStruct(near.shape, F32),) * 2,
        in_specs=[SMEM, VMEM, VMEM, VMEM, VMEM],
        out_specs=(VMEM, VMEM),
        compiler_params=params(4),
        cost_estimate=cost(100_000, 1_500_000),
        name="send_on",
    )(odd, near, far, keep, given)


def shifted(value, axis, step):
    count = lax.axis_size(axis)
    return lax.ppermute(value, axis, [(i, i + step) for i in range(count) if 0 <= i + step < count])


def other_core(value):
    return lax.ppermute(value, "tm", [(i, i ^ 1) for i in range(lax.axis_size("tm"))])


def windows(angle_index):
    theta = jnp.pi * angle_index.astype(F32) / ANGLES
    cosv, sinv = jnp.cos(theta), jnp.sin(theta)
    tile = jnp.arange(16)
    z0 = (16 * (tile // 2)).astype(F32) - 63.5
    y0 = (16 * (tile % 2)).astype(F32) - 15.5
    corner = y0[:, None] * cosv[None] + z0[:, None] * sinv[None] + 47.5
    least = corner + jnp.minimum(0.0, 15.0 * cosv)[None] + jnp.minimum(0.0, 15.0 * sinv)[None]
    base = jnp.floor(least - 0.001)
    return base.astype(jnp.int32).reshape(512), (corner - base).reshape(512), cosv, sinv


def on_device(
    trajectory,
    noise,
    start,
    conv_weight,
    conv_bias,
    step_embed,
    out_weight,
    decoder,
    angle_index,
    measured,
    step_scale,
    guide_scale,
    noise_scale,
):
    odd = (lax.axis_index("tm") % 2).reshape(1)
    xp, top, bottom, cum, tot, mm, wt, wo = prep(
        decoder, step_scale, guide_scale, measured, conv_weight, conv_bias, step_embed, out_weight, trajectory
    )
    up = shifted(top, "space", 1)
    down = shifted(bottom, "space", -1)
    other = other_core(tot)
    base, off, cosv, sinv = windows(angle_index)
    own = (step_scale, noise_scale, wt, wo, noise, start)
    (one,) = conv((1,), [xp], *own)
    both = tot + other
    parts = [other] + [shifted(both, "tm", 2 * i) for i in (1, 2, 3)]
    (two,) = conv((2,), [xp], *own, after=both)
    msg = message(step_scale, guide_scale, odd, cum, parts, mm, two)
    got = lax.all_to_all(msg.reshape(32, MSG, 128), "space", 0, 0, tiled=True)
    outer, keep, give = conv((0, 3), [xp, up, down], *own, (one, two), odd, msg)
    given = other_core(give)
    chip, got = add_then(keep, given, got)
    near = shifted(chip, "tm", 2)
    back = project(base, off, cosv, sinv, got.reshape(32 * MSG, 128))
    chips, back = add_then(chip, near, back)
    far = shifted(chips, "tm", 4)
    send, mine = send_on(odd, near, far, keep, given)
    theirs = other_core(send)
    back = lax.all_to_all(back.reshape(32, 16, 128), "space", 0, 0, tiled=True)
    return final(decoder, odd, back.reshape(512, 128), one, two, outer, mine, theirs)


def solution(mesh):
    return jax.shard_map(
        on_device,
        mesh=mesh,
        in_specs=(
            P("tm", None, "space", None, None),
            P("tm", None, "space", None, None),
            P(None, "space", None, None),
            P(),
            P(),
            P("tm", None),
            P(),
            P(),
            P(),
            P("space", None, None),
            P("tm"),
            P("tm"),
            P("tm"),
        ),
        out_specs=P("tm", None, "space", None, None),
        check_vma=False,
    )
```

```python
import functools

import jax
import jax.numpy as jnp
from jax import lax
from jax.experimental import pallas as pl
from jax.experimental.pallas import tpu as pltpu
from jax.sharding import PartitionSpec as P

ANGLES = 180
PROJ = 0.125
NV = 32
NS = 96
WIN = 24
PAD = 168
MSG = 24
F32 = jnp.float32
BF16 = jnp.bfloat16
VMEM = pl.BlockSpec(memory_space=pltpu.VMEM)
SMEM = pl.BlockSpec(memory_space=pltpu.SMEM)
ANY = pl.BlockSpec(memory_space=pl.ANY)
HBM = pl.BlockSpec(memory_space=pltpu.HBM)


def params(mib):
    return pltpu.CompilerParams(vmem_limit_bytes=mib << 20)


def in_hbm(*values):
    return [pltpu.with_memory_space_constraint(v, pltpu.HBM) for v in values]


def cost(flops, size, trans=0):
    return pl.CostEstimate(flops=flops, bytes_accessed=size, transcendentals=trans)


def conv_tables(cw, bias, embed, ow, wt, wo, tall):
    tall[...] = jnp.zeros_like(tall)
    for e in range(3):
        for a in range(3):
            for b in range(3):
                at = (e * 3 + a) * 48 + b * 8
                tall[at : at + 8, 0:64] = 0.5 * cw[9 * a + 3 * b + e].astype(F32)
    both = 0.5 * (bias[...].reshape(1, 64) + embed[...])
    hi = both.astype(BF16).astype(F32)
    mid = (both - hi).astype(BF16).astype(F32)
    for i, piece in enumerate((hi, mid, both - hi - mid)):
        tall[512 + 48 + 4 * i : 512 + 52 + 4 * i, 0:64] = piece
    flat = tall[0:512, :].T[:64]
    shift = tall[512:640, :].T[:64]
    shift = jnp.concatenate([jnp.zeros((64, 384), F32), shift], axis=1)
    for o in range(4):
        moved = flat if o == 0 else pltpu.roll(flat, 8 * o, 1)
        wt[o * 64 : o * 64 + 64, :] = (moved + shift)[:, :448].astype(BF16)
    out = ow[...].astype(F32)
    out = jnp.concatenate([out, out], axis=1)
    out = jnp.concatenate([out] * 4, axis=1)
    lane = lax.broadcasted_iota(jnp.int32, (8, 512), 1) // 64
    own = lane == lax.broadcasted_iota(jnp.int32, (8, 512), 0)
    for c in range(0, 8, 2):
        rows = [jnp.where(own, jnp.broadcast_to(out[i : i + 1], (8, 512)), 0.0) for i in (c, c + 1)]
        wo[c * 8 : c * 8 + 16, :] = jnp.concatenate(rows, axis=0).astype(BF16)


def prep_kernel(*refs):
    source = refs[8]
    xp, top, bottom, cum, tot, mm, wt, wo = refs[9:17]
    dec, scale, guide, meas, cw, bias, embed, ow, traj, sems, scr, tall = refs[17:]
    small = list(zip(refs[:8], (dec, scale, guide, meas, cw, bias, embed, ow)))
    small = [pltpu.make_async_copy(a, b, sems.at[4 + i]) for i, (a, b) in enumerate(small)]
    copies = [pltpu.make_async_copy(source.at[:, :, z], traj.at[z], sems.at[z]) for z in range(4)]
    for copy in copies + small:
        copy.start()
    for copy in small:
        copy.wait()
    conv_tables(cw, bias, embed, ow, wt, wo, tall)
    wk = [scale[k] * guide[k] for k in range(4)]
    mm[...] = jnp.zeros_like(mm)
    for s in range(3):
        x = meas[s]
        stack = jnp.concatenate([x] + [pltpu.roll(x, 128 - 32 * i, 1) for i in range(1, 4)], axis=0)
        mm[pl.ds(s, 32, stride=8), :] = stack.T[:32]
    for z in range(4):
        copies[z].wait()
        run = None
        for k in range(4):
            acc = None
            for c in range(8):
                v = traj[z, k, c].astype(F32)
                scr[k % 2, c * 32 : (c + 1) * 32, :] = v
                term = dec[c] * v
                acc = term if acc is None else acc + term
            acc = wk[k] * acc
            run = acc if run is None else run + acc
            cum[k, z * 16 : z * 16 + 16, :] = run[:16]
            cum[k, 64 + z * 16 : 64 + z * 16 + 16, :] = run[16:]
            for y in range(0, 32, 2):
                rows = jnp.concatenate(
                    [scr[k % 2, pl.ds(y, 8, stride=32), :], scr[k % 2, pl.ds(y + 1, 8, stride=32), :]], axis=0
                )
                rows = rows.astype(BF16)
                xp[k, z, y * 8 : y * 8 + 16, :] = rows
                if z == 0:
                    bottom[k, y * 8 : y * 8 + 16, :] = rows
                if z == 3:
                    top[k, y * 8 : y * 8 + 16, :] = rows
        tot[z * 16 : z * 16 + 16, :] = run[:16]
        tot[64 + z * 16 : 64 + z * 16 + 16, :] = run[16:]
    tot[128:136, :] = jnp.full((8, 128), wk[0] + wk[1] + wk[2] + wk[3], F32)


def prep(dec, scale, guide, meas, conv_weight, conv_bias, step_embed, out_weight, traj):
    conv_weight = conv_weight.swapaxes(1, 2)
    return pl.pallas_call(
        prep_kernel,
        out_shape=(
            jax.ShapeDtypeStruct((4, 4, 256, 128), BF16),
            jax.ShapeDtypeStruct((4, 256, 128), BF16),
            jax.ShapeDtypeStruct((4, 256, 128), BF16),
            jax.ShapeDtypeStruct((4, 128, 128), F32),
            jax.ShapeDtypeStruct((136, 128), F32),
            jax.ShapeDtypeStruct((256, 128), F32),
            jax.ShapeDtypeStruct((256, 448), BF16),
            jax.ShapeDtypeStruct((64, 512), BF16),
        ),
        in_specs=[HBM] * 9,
        out_specs=(VMEM,) * 8,
        scratch_shapes=[
            pltpu.SMEM((8,), F32),
            pltpu.SMEM((4,), F32),
            pltpu.SMEM((4,), F32),
            pltpu.VMEM((3, 32, 128), F32),
            pltpu.VMEM((27, 8, 64), BF16),
            pltpu.VMEM((64,), F32),
            pltpu.VMEM((4, 64), F32),
            pltpu.VMEM((8, 64), BF16),
            pltpu.VMEM((4, 4, 8, 32, 128), BF16),
            pltpu.SemaphoreType.DMA((12,)),
            pltpu.VMEM((2, 256, 128), F32),
            pltpu.VMEM((640, 128), F32),
        ],
        compiler_params=params(16),
        cost_estimate=cost(4_000_000, 2_600_000),
        name="prep",
    )(*in_hbm(dec, scale, guide, meas, conv_weight, conv_bias, step_embed, out_weight, traj))


def message_kernel(scale, guide, odd, cum, other, one, two, three, mm, after, msg):
    wk = [scale[k] * guide[k] for k in range(4)]
    before = jnp.where(odd[0] == 0, 0.0, other[...]) + (one[...] + two[...] + three[...])
    for k in range(4):
        flipped = (cum[k] + before[:128]).T
        for i in range(4):
            msg[pl.ds(4 * i + k, 32, stride=MSG), :] = flipped[32 * i : 32 * i + 32]
    sub = lax.broadcasted_iota(jnp.int32, (8, 128), 0)
    w = before[128:136]
    for k in range(4):
        w = w + jnp.where(sub % 4 >= k, wk[k], 0.0)
    for d in range(32):
        msg[d * MSG + 16 : d * MSG + 24, :] = jnp.where(sub >= 4, w, mm[d * 8 : d * 8 + 8, :])


def message(scale, guide, odd, cum, parts, mm, after):
    return pl.pallas_call(
        message_kernel,
        out_shape=jax.ShapeDtypeStruct((32 * MSG, 128), F32),
        in_specs=[SMEM, SMEM, SMEM] + [VMEM] * 6 + [ANY],
        out_specs=VMEM,
        compiler_params=params(8),
        cost_estimate=cost(100_000, 900_000),
        name="message",
    )(*in_hbm(scale, guide), odd, cum, *parts, mm, after)


def conv_kernel(zs, refs_of, ns_in, scale, nscale, *refs):
    ins, rest = list(refs[:ns_in]), refs[ns_in:]
    wt, wo, noise_from, start_from = rest[:4]
    extra = rest[4:]
    done = None
    fetched = {}
    if ns_in == 3:
        done_from, odd, extra = extra[:2], extra[2], extra[4:]
        run_ref, tot_ref, give_ref, scr, noise, start, sems, held_planes, done, begun, more_sems = extra
        sources = [ins[1], ins[0].at[:, 0], ins[0].at[:, 1], ins[0].at[:, 2], ins[0].at[:, 3], ins[2]]
        for p, source in enumerate(sources):
            fetched[p] = pltpu.make_async_copy(source, held_planes.at[p], more_sems.at[p])
            fetched[p].start()
        for i in range(2):
            fetched[6 + i] = pltpu.make_async_copy(done_from[i].at[3, :, 0], done.at[i], more_sems.at[6 + i])
            fetched[8 + i] = pltpu.make_async_copy(start_from.at[:, 1 + i], begun.at[i], more_sems.at[8 + i])
            fetched[6 + i].start()
            fetched[8 + i].start()
        ins = [held_planes]
    else:
        run_ref, scr, noise, start, sems = extra[1:] if len(extra) == 6 else extra

    def put(value, z, rows):
        if done is not None:
            low, high = value[:4], value[4:]
            tot_ref[:, z, rows, :] = jnp.where(odd[0] == 0, low, high)
            give_ref[:, z, rows, :] = jnp.where(odd[0] == 0, high, low)

    copies = []
    for i, z in enumerate(zs):
        copies.append(pltpu.make_async_copy(noise_from.at[:, :, z], noise.at[i], sems.at[0, i]))
        copies.append(pltpu.make_async_copy(start_from.at[:, z], start.at[i], sems.at[1, i]))
    for copy in copies:
        copy.start()
    planes = refs_of(ins)
    lane = lax.broadcasted_iota(jnp.int32, (16, 128), 1)
    zero = jnp.zeros((8, 128), BF16)
    for p, plane in enumerate(planes):
        if fetched:
            fetched[p].wait()
        for k in range(4):
            for e in range(3):
                scr[p, e, k, 0:16, :] = jnp.zeros((16, 128), BF16)
                scr[p, e, k, 256:272, :] = jnp.zeros((16, 128), BF16)
            held = zero.astype(F32)
            rows = plane(k)
            for r in range(17):
                if r < 16:
                    cur = rows(r).astype(F32)
                    v = jnp.concatenate([held, cur[:8]], axis=0)
                    held = cur[8:]
                else:
                    v = jnp.concatenate([held, zero.astype(F32)], axis=0)
                left = jnp.where(lane == 0, 0.0, pltpu.roll(v, 1, 1))
                right = jnp.where(lane == 127, 0.0, pltpu.roll(v, 127, 1))
                scr[p, 0, k, r * 16 : r * 16 + 16, :] = left.astype(BF16)
                scr[p, 1, k, r * 16 : r * 16 + 16, :] = v.astype(BF16)
                scr[p, 2, k, r * 16 : r * 16 + 16, :] = right.astype(BF16)
    row = lax.broadcasted_iota(jnp.int32, (16, 512), 0)
    kk = lax.broadcasted_iota(jnp.int32, (16, 512), 1) // 128
    ones = jnp.where((row < 12) & (row % 4 == kk), 1.0, 0.0).astype(BF16)

    lazy = len(zs) == 1
    if not lazy:
        for copy in copies:
            copy.wait()

    def block(step, carry):
        zi, yb = step // 2, step % 2
        first = 3 * zi
        zrow = pl.multiple_of(yb * 16, 16)
        for half in range(2):
            hidden = []
            for jj in range(2):
                top = pl.multiple_of((yb * 4 + half * 2 + jj) * 32, 32)
                parts = []
                for e in range(3):
                    for a in range(3):
                        parts.append(
                            jnp.concatenate([scr[first + a, e, k, pl.ds(top, 48), :] for k in range(4)], axis=1)
                        )
                parts.append(ones)
                patch = jnp.concatenate(parts, axis=0)
                pre = jnp.dot(wt[...], patch, preferred_element_type=F32)
                hidden.append((pre + pre * jnp.tanh(pre)).astype(BF16))
            eps = jnp.dot(wo[...], jnp.concatenate(hidden, axis=0), preferred_element_type=F32)
            at = pl.multiple_of(yb * 16 + half * 8, 8)
            if half == 0:
                if lazy:

                    @pl.when(step == 0)
                    def _():
                        for copy in copies:
                            copy.wait()

                grain = [noise[zi, k, :, pl.ds(zrow, 16), :].astype(F32) for k in range(4)]
                begin = start[zi, :, pl.ds(zrow, 16), :]
            acc = None
            for k in range(4):
                term = scale[k] * eps[:, k * 128 : k * 128 + 128].reshape(8, 8, 128)
                term = term + nscale[k] * grain[k][:, half * 8 : half * 8 + 8]
                acc = term if acc is None else acc + term
                run_ref[k, :, zi, pl.ds(at, 8), :] = acc + begin[:, half * 8 : half * 8 + 8]
            put(acc, 3 * zi, pl.ds(at, 8))
        return carry

    lax.fori_loop(0, 2 * len(zs), block, 0)
    if done is not None:
        for z in range(2):
            fetched[6 + z].wait()
            fetched[8 + z].wait()
            put(done[z] - begun[z], 1 + z, pl.ds(0, 32))


def conv(zs, planes, scale, nscale, wt, wo, noise, start, done=None, odd=None, after=None):
    inner = len(zs) == 1

    def refs_of(ins):
        own = ins[0]

        def of(z):
            if inner:
                return lambda k: (lambda r: own[k, zs[0] - 1 + z, r * 16 : r * 16 + 16, :])
            return lambda k: (lambda r: own[z, k, r * 16 : r * 16 + 16, :])

        return [of(z) for z in range(3 * len(zs))]

    more = [] if after is None else [after]
    more = more if done is None else [*done, odd, after]
    extra = []
    if not inner:
        planes = in_hbm(*planes)
        extra = [
            pltpu.VMEM((6, 4, 256, 128), BF16),
            pltpu.VMEM((2, 8, 32, 128), F32),
            pltpu.VMEM((2, 8, 32, 128), F32),
            pltpu.SemaphoreType.DMA((10,)),
        ]
    sums = []
    if done is not None:
        sums = [jax.ShapeDtypeStruct((4, 4, 32, 128), F32)] * 2
    return pl.pallas_call(
        functools.partial(conv_kernel, zs, refs_of, len(planes)),
        out_shape=(
            jax.ShapeDtypeStruct((4, 8, len(zs), 32, 128), F32),
            *sums,
        ),
        in_specs=[SMEM, SMEM]
        + [VMEM if inner else HBM] * len(planes)
        + [VMEM, VMEM, HBM, HBM]
        + ([ANY, ANY, SMEM, ANY] if done is not None else [ANY] * len(more)),
        out_specs=(VMEM,) * (1 + len(sums)),
        scratch_shapes=[
            pltpu.VMEM((3 * len(zs), 3, 4, 272, 128), BF16),
            pltpu.VMEM((len(zs), 4, 8, 32, 128), BF16),
            pltpu.VMEM((len(zs), 8, 32, 128), F32),
            pltpu.SemaphoreType.DMA((2, 2)),
            *extra,
        ],
        compiler_params=params(16),
        cost_estimate=cost(3_000_000_000 * len(zs), 2_000_000 * len(zs), 1_000_000 * len(zs)),
        name=f"conv_{zs[0]}" if inner else "conv_outer",
    )(*in_hbm(scale, nscale), *planes, wt, wo, *in_hbm(noise, start), *more)


def project_kernel(base, off, cosv, sinv, got, out, table, sino, meas, seen_hi, seen_lo):
    lane = lax.broadcasted_iota(jnp.int32, (16, 128), 1)
    low = lane < 64
    sino[...] = jnp.zeros_like(sino)
    for d in range(32):
        meas[3 * d : 3 * d + 3, :] = got[d * MSG + 16 : d * MSG + 19, :]
    cell = lax.broadcasted_iota(jnp.int32, (8, 256), 1)
    dy = (cell % 16).astype(F32)
    dz = (cell // 16).astype(F32)
    sub = lax.broadcasted_iota(jnp.int32, (8, 256), 0).astype(F32)

    def where_rows(t, v):
        return v * PAD + 24 + base[t * NV + v]

    def forward(zt, carry):
        slab = [got[pl.ds(pl.multiple_of((4 * zt + i) * MSG, 8), 16), :] for i in range(4)]
        flip = [pltpu.roll(s, 64, 1) for s in slab]
        tiles = [
            jnp.concatenate([jnp.where(low, slab[0], flip[1]), jnp.where(low, slab[2], flip[3])], axis=1),
            jnp.concatenate([jnp.where(low, flip[0], slab[1]), jnp.where(low, flip[2], slab[3])], axis=1),
        ]
        for yt in range(2):
            t = zt * 2 + yt
            image = tiles[yt]
            hi = image.astype(BF16)
            lo = (image - hi.astype(F32)).astype(BF16)
            gap = jnp.zeros((16, 256), BF16)
            columns = jnp.concatenate([gap, gap, hi, gap, lo, gap, gap, gap], axis=0)
            columns = jnp.concatenate([columns, columns], axis=1)
            for v in range(0, NV, 2):
                rows = []
                for u in (v, v + 1):
                    at = dy * cosv[u] + dz * sinv[u] + off[t * NV + u]
                    for b in range(3):
                        rows.append(jnp.maximum(0.0, 1.0 - jnp.abs(at - (sub + 8.0 * b))))
                hat = jnp.concatenate(rows, axis=0)
                top = hat.astype(BF16)
                rest = (hat - top.astype(F32)).astype(BF16)
                table[t, v * WIN : (v + 2) * WIN, 0:256] = top
                table[t, v * WIN : (v + 2) * WIN, 256:512] = rest
            sums = lax.dot_general(table[t], columns, (((1,), (1,)), ((), ())), preferred_element_type=F32)
            for v in range(NV):
                at = pl.ds(where_rows(t, v), WIN)
                sino[at, :] = sino[at, :] + sums[v * WIN : (v + 1) * WIN]
        return carry

    lax.fori_loop(0, 8, forward, 0, unroll=2)

    whole = meas[...]
    whole_hi = whole.astype(BF16).astype(F32)
    seen_hi[...] = whole_hi
    seen_lo[...] = pltpu.roll(whole - whole_hi, 1, 1)
    wide = lax.broadcasted_iota(jnp.int32, (8, 128), 1)
    is_hi = (wide >= 32) & (wide < 48)
    is_lo = (wide >= 64) & (wide < 80)
    is_seen = wide % 32 == 24
    is_rest = wide % 32 == 25

    def misfit(v):
        at = pl.multiple_of(v * PAD, 8)
        turn = lax.rem(128 + 24 - v, 128)
        for r in range(0, NS, 8):
            rows = sino[pl.ds(at + 24 + r, 8), :]
            rows = PROJ * (rows + pltpu.roll(rows, 96, 1))
            hi = rows.astype(BF16).astype(F32)
            lo = pltpu.roll(rows - hi, 32, 1)
            top = pltpu.roll(seen_hi[r : r + 8, :], turn, 1)
            rest = pltpu.roll(seen_lo[r : r + 8, :], turn, 1)
            spread = jnp.where(is_hi, hi, jnp.where(is_lo, lo, 0.0))
            sino[pl.ds(at + 24 + r, 8), :] = jnp.where(is_seen, top, jnp.where(is_rest, rest, spread))
        sino[pl.ds(at, 24), :] = jnp.zeros((24, 128), F32)
        sino[pl.ds(at + 120, 48), :] = jnp.zeros((48, 128), F32)

    def misfits(group, carry):
        for v in range(16):
            misfit(group * 16 + v)
        return carry

    lax.fori_loop(0, NV // 16, misfits, 0)

    upper = lax.broadcasted_iota(jnp.int32, (8, 256), 0) < 4
    wk = got[16:24, :]
    wk = jnp.where(upper[:, :128], pltpu.roll(wk, 4, 0), wk)
    wk = jnp.concatenate([wk, wk], axis=1)

    def backward(zt, carry):
        tiles = []
        for yt in range(2):
            t = zt * 2 + yt
            rows = jnp.concatenate([sino[pl.ds(where_rows(t, v), WIN), :] for v in range(NV)], axis=0)
            sums = lax.dot_general(
                rows.astype(BF16), table[t], (((0,), (0,)), ((), ())), preferred_element_type=F32
            )
            sums = sums[:, :256] + sums[:, 256:]
            pair = []
            for h in range(2):
                seen = [
                    sums[24 + 32 * i : 25 + 32 * i] + sums[25 + 32 * i : 26 + 32 * i] for i in (2 * h, 2 * h + 1)
                ]
                ours = sums[32 + 8 * h : 40 + 8 * h] + sums[64 + 8 * h : 72 + 8 * h]
                pair.append(PROJ * (ours - wk * jnp.where(upper, seen[0], seen[1])))
            tiles.append(jnp.concatenate(pair, axis=0))
        for h in range(2):
            a, b = (tile[:, 128 * h : 128 * h + 128] for tile in tiles)
            at = pl.multiple_of((4 * zt + 2 * h) * 16, 16)
            out[pl.ds(at, 16), :] = jnp.where(low, a, pltpu.roll(b, 64, 1))
            out[pl.ds(at + 16, 16), :] = jnp.where(low, pltpu.roll(a, 64, 1), b)
        return carry

    lax.fori_loop(0, 8, backward, 0, unroll=4)


def project(base, off, cosv, sinv, got):
    return pl.pallas_call(
        project_kernel,
        out_shape=jax.ShapeDtypeStruct((512, 128), F32),
        in_specs=[SMEM, SMEM, SMEM, SMEM, VMEM],
        out_specs=VMEM,
        scratch_shapes=[
            pltpu.VMEM((16, NV * WIN, 512), BF16),
            pltpu.VMEM((NV * PAD, 128), F32),
            pltpu.VMEM((NS, 128), F32),
            pltpu.VMEM((NS, 128), F32),
            pltpu.VMEM((NS, 128), F32),
        ],
        compiler_params=params(22),
        cost_estimate=cost(8_000_000_000, 2_000_000),
        name="project",
    )(base, off, cosv, sinv, got)


def final_kernel(dec, odd, back, one, two, outer, mine_from, theirs_from, new, held, mine, theirs, sems):
    parts = [
        pltpu.make_async_copy(mine_from, mine, sems.at[4]),
        pltpu.make_async_copy(theirs_from, theirs, sems.at[5]),
    ]
    for part in parts:
        part.start()
    copies = []
    for k in range(4):
        columns = jnp.concatenate([back[pl.ds(4 * i + k, 32, stride=16), :] for i in range(4)], axis=0)
        cells = columns.T
        if k == 0:
            for part in parts:
                part.wait()
        for z in range(4):
            guide = jnp.concatenate([cells[z * 16 : z * 16 + 16], cells[64 + z * 16 : 80 + z * 16]], axis=0)
            for c in range(8):
                own = (one, two)[z - 1][k, c, 0] if z in (1, 2) else outer[k, c, z // 3]
                before = jnp.where(odd[0] == c // 4, mine[c % 4, z], theirs[c % 4, z])
                held[k, c, z] = own + before - dec[c] * guide
        copies.append(pltpu.make_async_copy(held.at[k], new.at[k], sems.at[k]))
        copies[k].start()
    for copy in copies:
        copy.wait()


def final(dec, odd, back, one, two, outer, mine, theirs):
    return pl.pallas_call(
        final_kernel,
        out_shape=jax.ShapeDtypeStruct((4, 8, 4, 32, 128), F32),
        in_specs=[SMEM, SMEM] + [VMEM] * 4 + [ANY, ANY],
        out_specs=HBM,
        scratch_shapes=[
            pltpu.VMEM((4, 8, 4, 32, 128), F32),
            pltpu.VMEM((4, 4, 32, 128), F32),
            pltpu.VMEM((4, 4, 32, 128), F32),
            pltpu.SemaphoreType.DMA((6,)),
        ],
        compiler_params=params(8),
        cost_estimate=cost(2_000_000, 5_000_000),
        name="final",
    )(*in_hbm(dec), odd, back, one, two, outer, *in_hbm(mine), theirs)


def add_kernel(a, b, held, out, passed):
    out[...] = a[...] + b[...]


def add_then(a, b, held):
    return pl.pallas_call(
        add_kernel,
        out_shape=(jax.ShapeDtypeStruct(a.shape, F32), jax.ShapeDtypeStruct(held.shape, held.dtype)),
        in_specs=[VMEM, VMEM, ANY],
        out_specs=(VMEM, ANY),
        input_output_aliases={2: 1},
        compiler_params=params(4),
        cost_estimate=cost(100_000, 800_000),
        name="add_then",
    )(a, b, held)


def send_kernel(odd, near, far, keep, given, send, mine):
    first = odd[0] == 0
    chips = near[...] + far[...]
    send[...] = chips + jnp.where(first, keep[...], 0.0)
    mine[...] = chips + jnp.where(first, 0.0, given[...])


def send_on(odd, near, far, keep, given):
    return pl.pallas_call(
        send_kernel,
        out_shape=(jax.ShapeDtypeStruct(near.shape, F32),) * 2,
        in_specs=[SMEM, VMEM, VMEM, VMEM, VMEM],
        out_specs=(VMEM, VMEM),
        compiler_params=params(4),
        cost_estimate=cost(100_000, 1_500_000),
        name="send_on",
    )(odd, near, far, keep, given)


def shifted(value, axis, step):
    count = lax.axis_size(axis)
    return lax.ppermute(value, axis, [(i, i + step) for i in range(count) if 0 <= i + step < count])


def other_core(value):
    return lax.ppermute(value, "tm", [(i, i ^ 1) for i in range(lax.axis_size("tm"))])


def windows(angle_index):
    theta = jnp.pi * angle_index.astype(F32) / ANGLES
    cosv, sinv = jnp.cos(theta), jnp.sin(theta)
    tile = jnp.arange(16)
    z0 = (16 * (tile // 2)).astype(F32) - 63.5
    y0 = (16 * (tile % 2)).astype(F32) - 15.5
    corner = y0[:, None] * cosv[None] + z0[:, None] * sinv[None] + 47.5
    least = corner + jnp.minimum(0.0, 15.0 * cosv)[None] + jnp.minimum(0.0, 15.0 * sinv)[None]
    base = jnp.floor(least - 0.001)
    return base.astype(jnp.int32).reshape(512), (corner - base).reshape(512), cosv, sinv


def on_device(
    trajectory,
    noise,
    start,
    conv_weight,
    conv_bias,
    step_embed,
    out_weight,
    decoder,
    angle_index,
    measured,
    step_scale,
    guide_scale,
    noise_scale,
):
    odd = (lax.axis_index("tm") % 2).reshape(1)
    xp, top, bottom, cum, tot, mm, wt, wo = prep(
        decoder, step_scale, guide_scale, measured, conv_weight, conv_bias, step_embed, out_weight, trajectory
    )
    up = shifted(top, "space", 1)
    down = shifted(bottom, "space", -1)
    other = other_core(tot)
    base, off, cosv, sinv = windows(angle_index)
    own = (step_scale, noise_scale, wt, wo, noise, start)
    (one,) = conv((1,), [xp], *own)
    both = tot + other
    parts = [other] + [shifted(both, "tm", 2 * i) for i in (1, 2, 3)]
    (two,) = conv((2,), [xp], *own, after=both)
    msg = message(step_scale, guide_scale, odd, cum, parts, mm, two)
    got = lax.all_to_all(msg.reshape(32, MSG, 128), "space", 0, 0, tiled=True)
    outer, keep, give = conv((0, 3), [xp, up, down], *own, (one, two), odd, msg)
    given = other_core(give)
    chip, got = add_then(keep, given, got)
    near = shifted(chip, "tm", 2)
    back = project(base, off, cosv, sinv, got.reshape(32 * MSG, 128))
    chips, back = add_then(chip, near, back)
    far = shifted(chips, "tm", 4)
    send, mine = send_on(odd, near, far, keep, given)
    theirs = other_core(send)
    back = lax.all_to_all(back.reshape(32, 16, 128), "space", 0, 0, tiled=True)
    return final(decoder, odd, back.reshape(512, 128), one, two, outer, mine, theirs)


def solution(mesh):
    return jax.shard_map(
        on_device,
        mesh=mesh,
        in_specs=(
            P("tm", None, "space", None, None),
            P("tm", None, "space", None, None),
            P(None, "space", None, None),
            P(),
            P(),
            P("tm", None),
            P(),
            P(),
            P(),
            P("space", None, None),
            P("tm"),
            P("tm"),
            P("tm"),
        ),
        out_specs=P("tm", None, "space", None, None),
        check_vma=False,
    )
```
